32 devices in a mesh: src: 8 (over y, x, core), tgt: 4 (over z).
Axes of the slice: x: 2, y: 2, z: 4, core: 2. Of those that a mesh axis runs over, the one named last changes fastest.
Arguments:
- feat_in: bfloat16 [32, 49, 128], P(('src', 'tgt')), may hold values from -6 to 6
- ffn_in: bfloat16 [32, 49, 128], P(('src', 'tgt')), may hold values from -6 to 6
- grad_out: bfloat16 [32, 49, 128], P(('src', 'tgt')), may hold values from -6 to 6
- ffn_up: bfloat16 [128, 512], replicated, may hold values from -0.5 to 0.5
- ffn_down: bfloat16 [512, 128], replicated, may hold values from -0.25 to 0.25
- so2_zero: bfloat16 [896, 1024], P('tgt'), may hold values from -0.1875 to 0.1875
- so2_one: bfloat16 [2, 768, 768], P(None, 'tgt'), may hold values from -0.15625 to 0.15625
- so2_two: bfloat16 [2, 640, 640], P(None, 'tgt'), may hold values from -0.15625 to 0.15625
- wigner: bfloat16 [64, 29, 49], replicated, may hold values from -1 to 1
- edge_src: int32 [8, 4, 128], P('src', 'tgt'), may hold values from 0 to 3
- edge_tgt: int32 [8, 4, 128], P('src', 'tgt'), may hold values from 0 to 7
- edge_angle: int32 [8, 4, 128], P('src', 'tgt'), may hold values from 0 to 63
- edge_radial: bfloat16 [8, 4, 128, 128], P('src', 'tgt'), may hold values from 0.25 to 2
- edge_count: int32 [8, 4], P('src', 'tgt'), may hold values from 1 to 128, as said below
Outputs:
- feat_grad: bfloat16 [32, 49, 128], P(('src', 'tgt'))
The draws below stay inside these ranges and needn't reach their ends.
Inputs may be any that keep to these rules, and one draw needn't show every extreme that they name: The slots of a block at or past its edge_count are padding. Some block holds 128 edges.
All inputs are finite; a program needn't handle non-finite values.
Results may differ from the reference program's by a relative error of at most 0.006.
Values may be sent and summed in bfloat16 or wider, within the bound.
A program may use at most 64 MiB of HBM per device.

```python
import math
import jax
import jax.numpy as jnp
import numpy as np
from jax import lax

C = 128
HID = 512
LMAX = 6
GRID_SIDE = 14
N_ANG = 64
ATOM_DEV = 1
E_CAP = 128
COEF = 49
KEEP = 29
SRC_GRP = 4
TGT_GRP = 8
ATOMS = 32
N_SRC = 8
N_TGT = 4


def draw_wigner(key, part):
    rotations = jnp.zeros((N_ANG, KEEP, COEF), jnp.float32)
    blocks = []
    for degree in range(LMAX + 1):
        width_here = 2 * degree + 1
        gaussian = jax.random.normal(jax.random.fold_in(key, 11 + degree), (N_ANG, width_here, width_here), jnp.float32)
        blocks.append(jnp.linalg.qr(gaussian)[0])
    row_index = 0
    for order_m in [0, 1, -1, 2, -2]:
        for degree in range(abs(order_m), LMAX + 1):
            rotations = rotations.at[:, row_index, degree * degree:(degree + 1) * (degree + 1)].set(blocks[degree][:, degree + order_m, :])
            row_index = row_index + 1
    return rotations.astype(jnp.bfloat16)


def draw_edge_count(key, part):
    levels = jax.random.randint(jax.random.fold_in(key, 31), (N_SRC * N_TGT,), 0, 16)
    chosen = jax.random.randint(jax.random.fold_in(key, 32), (), 0, N_SRC * N_TGT)
    levels = jnp.where(jnp.arange(N_SRC * N_TGT) == chosen, 15, levels)
    counts = 1 + (E_CAP - 1) * (levels + 1) * (levels + 1) // 256
    return counts.reshape(N_SRC, N_TGT).astype(jnp.int32)


def with_ends(drawn, own_key, smallest, top_value):
    index_at = [jax.random.randint(jax.random.fold_in(own_key, axis), (), 0, length) for axis, length in enumerate(drawn.shape)]
    longest = drawn.shape.index(max(drawn.shape))
    neighbour = index_at[:longest] + [(index_at[longest] + 1) % drawn.shape[longest]] + index_at[longest + 1:]
    return drawn.at[tuple(index_at)].set(smallest).at[tuple(neighbour)].set(top_value)


def level_of(stream_key, shape, split, smallest, high):
    def one(position, blocks):
        steps = jax.random.uniform(jax.random.fold_in(jax.random.fold_in(stream_key, 6), position), (blocks,), jnp.float32, smallest / len(split), high / len(split))
        return jnp.repeat(jnp.exp(steps), shape[position] // blocks).reshape((-1,) + (1,) * (len(shape) - position - 1))

    factor_of = one(*split[0])
    for cut in split[1:]:
        factor_of = factor_of * one(*cut)
    return factor_of


def bell_draw(key, extent, deviation, bound, pieces=(), held_as=jnp.bfloat16):
    array = deviation * jax.random.normal(key, extent, jnp.float32)
    if pieces:
        array = array * level_of(key, extent, pieces, -0.22, 0.18)
    return jnp.clip(array, -bound, bound).astype(held_as)


def setup_inputs(seed: int = 0) -> dict:
    seeds = jax.random.split(jax.random.key(seed), 15)
    return {
        "feat_in": bell_draw(seeds[0], (ATOMS, COEF, C), 1.0, 6.0, ((0, 32),)),
        "ffn_in": bell_draw(seeds[1], (ATOMS, COEF, C), 1.0, 6.0, ((0, 32),)),
        "grad_out": bell_draw(seeds[2], (ATOMS, COEF, C), 1.0, 6.0, ((0, 32),)),
        "ffn_up": bell_draw(seeds[3], (C, HID), C ** -0.5, 0.5),
        "ffn_down": bell_draw(seeds[4], (HID, C), HID ** -0.5, 0.25),
        "so2_zero": bell_draw(seeds[5], ((LMAX + 1) * C, (LMAX + 2) * C), ((LMAX + 1) * C) ** -0.5, 0.1875, ((0, 4),)),
        "so2_one": bell_draw(seeds[6], (2, LMAX * C, LMAX * C), (2 * LMAX * C) ** -0.5, 0.15625, ((1, 4),)),
        "so2_two": bell_draw(seeds[7], (2, (LMAX - 1) * C, (LMAX - 1) * C), (2 * (LMAX - 1) * C) ** -0.5, 0.15625, ((1, 4),)),
        "wigner": draw_wigner(jax.random.fold_in(seeds[14], 71), 0),
        "edge_src": with_ends(jax.random.randint(seeds[9], (N_SRC, N_TGT, E_CAP), 0, SRC_GRP), jax.random.fold_in(seeds[9], 1), 0, SRC_GRP - 1).astype(jnp.int32),
        "edge_tgt": with_ends(jax.random.randint(seeds[10], (N_SRC, N_TGT, E_CAP), 0, TGT_GRP), jax.random.fold_in(seeds[10], 1), 0, TGT_GRP - 1).astype(jnp.int32),
        "edge_angle": with_ends(jax.random.randint(seeds[11], (N_SRC, N_TGT, E_CAP), 0, N_ANG), jax.random.fold_in(seeds[11], 1), 0, N_ANG - 1).astype(jnp.int32),
        "edge_radial": jnp.clip(jnp.exp(math.log(2.0) - 2.0794415 * jax.random.uniform(seeds[12], (N_SRC, N_TGT, E_CAP, C), jnp.float32) ** level_of(seeds[12], (N_SRC, N_TGT, E_CAP, C), ((0, 8), (1, 4)), -0.2, 0.2)), 0.25, 2.0).astype(jnp.bfloat16),
        "edge_count": draw_edge_count(jax.random.fold_in(seeds[14], 71), 0),
    }


message_scale = 0.125

def sphere_tables(degree_max, grid_side):
    polar_angle = (np.arange(grid_side) + 0.5) * np.pi / grid_side
    azimuth = np.arange(grid_side) * 2.0 * np.pi / grid_side
    cosine = np.cos(polar_angle)
    sine_theta = np.sin(polar_angle)
    coef_count = (degree_max + 1) * (degree_max + 1)
    harmonics = np.zeros((grid_side, grid_side, coef_count))
    for order_m in range(degree_max + 1):
        diagonal = np.ones(grid_side)
        for factor in range(1, order_m + 1):
            diagonal = diagonal * (2 * factor - 1) * sine_theta
        legendre = {order_m: diagonal}
        if order_m + 1 <= degree_max:
            legendre[order_m + 1] = cosine * (2 * order_m + 1) * diagonal
        for degree in range(order_m + 2, degree_max + 1):
            legendre[degree] = ((2 * degree - 1) * cosine * legendre[degree - 1] - (degree + order_m - 1) * legendre[degree - 2]) / (degree - order_m)
        for degree in range(order_m, degree_max + 1):
            scaling = math.sqrt((2 * degree + 1) / (4.0 * math.pi) * math.factorial(degree - order_m) / math.factorial(degree + order_m))
            if order_m > 0:
                scaling = scaling * math.sqrt(2.0)
            polar_part = scaling * legendre[degree]
            centre = degree * degree + degree
            harmonics[:, :, centre + order_m] = polar_part[:, None] * np.cos(order_m * azimuth)[None, :]
            if order_m > 0:
                harmonics[:, :, centre - order_m] = polar_part[:, None] * np.sin(order_m * azimuth)[None, :]
    to_grid = harmonics.reshape(grid_side * grid_side, coef_count)
    quadrature = np.repeat(sine_theta * (np.pi / grid_side) * (2.0 * np.pi / grid_side), grid_side)
    from_grid = (to_grid * quadrature[:, None]).T
    return (jnp.asarray(to_grid, jnp.float32).astype(jnp.bfloat16), jnp.asarray(from_grid, jnp.float32).astype(jnp.bfloat16))

def ffn_backward(ffn_rows, grad_rows, ffn_up, ffn_down, to_grid, from_grid):
    atom_count, coef_count, channels = ffn_rows.shape
    grid_feat = jnp.einsum('pk,akc->apc', to_grid.astype(jnp.float32), ffn_rows.astype(jnp.float32)).astype(jnp.bfloat16)
    grid_points = grid_feat.shape[1]
    pre_act = jnp.dot(grid_feat.reshape(atom_count * grid_points, channels).astype(jnp.float32), ffn_up.astype(jnp.float32), preferred_element_type=jnp.float32)
    grad_value = jnp.einsum('kp,akc->apc', from_grid.astype(jnp.float32), grad_rows.astype(jnp.float32)).astype(jnp.bfloat16)
    grad_act = jnp.dot(grad_value.reshape(atom_count * grid_points, channels).astype(jnp.float32), ffn_down.T.astype(jnp.float32), preferred_element_type=jnp.float32)
    sigmoid_pre = jax.nn.sigmoid(pre_act)
    grad_pre = (grad_act * sigmoid_pre * (1.0 + pre_act * (1.0 - sigmoid_pre))).astype(jnp.bfloat16)
    grad_grid = jnp.dot(grad_pre.astype(jnp.float32), ffn_up.T.astype(jnp.float32), preferred_element_type=jnp.float32).astype(jnp.bfloat16)
    ffn_term = jnp.einsum('pk,apc->akc', to_grid.astype(jnp.float32), grad_grid.reshape(atom_count, grid_points, channels).astype(jnp.float32))
    return (grad_rows.astype(jnp.float32) + ffn_term).astype(jnp.bfloat16)

def matmul_plain(left, right):
    return jnp.dot(left.astype(jnp.float32), right.astype(jnp.float32), preferred_element_type=jnp.float32)

def matmul_flip(left, right):
    return jnp.dot(left.astype(jnp.float32), right.T.astype(jnp.float32), preferred_element_type=jnp.float32)

def so2_forward(rotated, w_zero, w_one, w_two, degree_max, channels):
    cut_a = (degree_max + 1) * channels
    cut_b = cut_a + degree_max * channels
    cut_c = cut_b + degree_max * channels
    cut_d = cut_c + (degree_max - 1) * channels
    zero_part = rotated[:, :cut_a]
    one_plus = rotated[:, cut_a:cut_b]
    one_minus = rotated[:, cut_b:cut_c]
    two_plus = rotated[:, cut_c:cut_d]
    two_minus = rotated[:, cut_d:]
    out_zero = matmul_plain(zero_part, w_zero)
    out_one_plus = matmul_plain(one_plus, w_one[0]) - matmul_plain(one_minus, w_one[1])
    out_one_minus = matmul_plain(one_minus, w_one[0]) + matmul_plain(one_plus, w_one[1])
    out_two_plus = matmul_plain(two_plus, w_two[0]) - matmul_plain(two_minus, w_two[1])
    out_two_minus = matmul_plain(two_minus, w_two[0]) + matmul_plain(two_plus, w_two[1])
    return jnp.concatenate([out_zero, out_one_plus, out_one_minus, out_two_plus, out_two_minus], axis=1)

def so2_backward(grad_pre, w_zero, w_one, w_two, degree_max, channels):
    cut_a = (degree_max + 2) * channels
    cut_b = cut_a + degree_max * channels
    cut_c = cut_b + degree_max * channels
    cut_d = cut_c + (degree_max - 1) * channels
    grad_zero = grad_pre[:, :cut_a]
    grad_one_plus = grad_pre[:, cut_a:cut_b]
    grad_one_minus = grad_pre[:, cut_b:cut_c]
    grad_two_plus = grad_pre[:, cut_c:cut_d]
    grad_two_minus = grad_pre[:, cut_d:]
    back_zero = matmul_flip(grad_zero, w_zero)
    back_one_plus = matmul_flip(grad_one_plus, w_one[0]) + matmul_flip(grad_one_minus, w_one[1])
    back_one_minus = matmul_flip(grad_one_minus, w_one[0]) - matmul_flip(grad_one_plus, w_one[1])
    back_two_plus = matmul_flip(grad_two_plus, w_two[0]) + matmul_flip(grad_two_minus, w_two[1])
    back_two_minus = matmul_flip(grad_two_minus, w_two[0]) - matmul_flip(grad_two_plus, w_two[1])
    return jnp.concatenate([back_zero, back_one_plus, back_one_minus, back_two_plus, back_two_minus], axis=1)

def gate_backward(hidden, grad_o, degree_max):
    gate_index = degree_max + 1
    scalar_pre = hidden[:, 0]
    gate_pre = hidden[:, gate_index]
    sigmoid_gate = jax.nn.sigmoid(gate_pre)
    sigmoid_scalar = jax.nn.sigmoid(scalar_pre)
    grad_scalar = grad_o[:, 0] * sigmoid_scalar * (1.0 + scalar_pre * (1.0 - sigmoid_scalar))
    gated_rows = jnp.concatenate([hidden[:, 1:gate_index], hidden[:, gate_index + 1:]], axis=1)
    grad_rows = grad_o[:, 1:]
    grad_gate = lax.optimization_barrier(jnp.sum(grad_rows * gated_rows, axis=1)) * sigmoid_gate * (1.0 - sigmoid_gate)
    grad_gated = grad_rows * sigmoid_gate[:, None, :]
    return jnp.concatenate([grad_scalar[:, None], grad_gated[:, :degree_max], grad_gate[:, None], grad_gated[:, degree_max:]], axis=1)

def block_grad(source_group, target_group, src_ids, tgt_ids, angle_ids, radial, live_count, so2_zero, so2_one, so2_two, wigner):
    slot_count = src_ids.shape[0]
    rotation = wigner[angle_ids].astype(jnp.float32)
    source_rows = source_group[src_ids].astype(jnp.float32)
    rotated = jnp.einsum('erk,ekc->erc', rotation, source_rows).astype(jnp.bfloat16)
    hidden = so2_forward(rotated.reshape(slot_count, KEEP * C), so2_zero, so2_one, so2_two, LMAX, C)
    radial_gain = radial.astype(jnp.float32)[:, None, :]
    hidden = hidden.reshape(slot_count, KEEP + 1, C) * radial_gain
    target_rows = target_group[tgt_ids].astype(jnp.float32)
    grad_o = jnp.einsum('erk,ekc->erc', rotation, target_rows) * message_scale
    grad_hidden = gate_backward(hidden, grad_o, LMAX)
    grad_pre = (grad_hidden * radial_gain).astype(jnp.bfloat16).reshape(slot_count, (KEEP + 1) * C)
    grad_rot = so2_backward(grad_pre, so2_zero, so2_one, so2_two, LMAX, C).astype(jnp.bfloat16).reshape(slot_count, KEEP, C)
    grad_edge = jnp.einsum('erk,erc->ekc', rotation, grad_rot.astype(jnp.float32)).astype(jnp.bfloat16)
    live_slot = jnp.arange(slot_count, dtype=jnp.int32) < live_count
    masked = jnp.where(live_slot[:, None, None], grad_edge.astype(jnp.float32), jnp.zeros((), jnp.float32))
    return jax.ops.segment_sum(masked, src_ids, num_segments=SRC_GRP)

def reference(feat_in, ffn_in, grad_out, ffn_up, ffn_down, so2_zero, so2_one, so2_two, wigner, edge_src, edge_tgt, edge_angle, edge_radial, edge_count):
    to_grid, from_grid = sphere_tables(LMAX, GRID_SIDE)

    def ffn_group(group_items):
        return ffn_backward(group_items[0], group_items[1], ffn_up, ffn_down, to_grid, from_grid)
    target_grad = lax.map(ffn_group, (ffn_in.reshape(N_SRC, SRC_GRP, COEF, C), grad_out.reshape(N_SRC, SRC_GRP, COEF, C)))
    target_grad = target_grad.reshape(ATOMS, COEF, C)
    source_groups = feat_in.reshape(N_SRC, SRC_GRP, COEF, C)
    target_groups = target_grad.reshape(N_SRC, N_TGT, ATOM_DEV, COEF, C).transpose(1, 0, 2, 3, 4).reshape(N_TGT, TGT_GRP, COEF, C)

    def per_source(group_items):
        source_group, src_row, tgt_row, angle_row, radial_row, count_row = group_items

        def per_target(running, block_items):
            target_group, src_ids, tgt_ids, angle_ids, radial, live_count = block_items
            return (running + block_grad(source_group, target_group, src_ids, tgt_ids, angle_ids, radial, live_count, so2_zero, so2_one, so2_two, wigner), None)
        running, unused = lax.scan(per_target, jnp.zeros((SRC_GRP, COEF, C), jnp.float32), (target_groups, src_row, tgt_row, angle_row, radial_row, count_row))
        return running
    summed = lax.map(per_source, (source_groups, edge_src, edge_tgt, edge_angle, edge_radial, edge_count))
    return (target_grad.astype(jnp.float32) + summed.reshape(ATOMS, COEF, C)).astype(jnp.bfloat16)
```

```python
import functools
import math

import jax
import jax.numpy as jnp
import numpy as np
from jax import lax
from jax.experimental import pallas as pl
from jax.experimental.pallas import tpu as pltpu
from jax.sharding import PartitionSpec as P

LMAX = 6
GRID_SIDE = 14


message_scale = 0.125


def sphere_tables(degree_max, grid_side):
    polar_angle = (np.arange(grid_side) + 0.5) * np.pi / grid_side
    azimuth = np.arange(grid_side) * 2.0 * np.pi / grid_side
    cosine = np.cos(polar_angle)
    sine_theta = np.sin(polar_angle)
    coef_count = (degree_max + 1) * (degree_max + 1)
    harmonics = np.zeros((grid_side, grid_side, coef_count))
    for order_m in range(degree_max + 1):
        diagonal = np.ones(grid_side)
        for factor in range(1, order_m + 1):
            diagonal = diagonal * (2 * factor - 1) * sine_theta
        legendre = {order_m: diagonal}
        if order_m + 1 <= degree_max:
            legendre[order_m + 1] = cosine * (2 * order_m + 1) * diagonal
        for degree in range(order_m + 2, degree_max + 1):
            legendre[degree] = (
                (2 * degree - 1) * cosine * legendre[degree - 1]
                - (degree + order_m - 1) * legendre[degree - 2]
            ) / (degree - order_m)
        for degree in range(order_m, degree_max + 1):
            scaling = math.sqrt(
                (2 * degree + 1)
                / (4.0 * math.pi)
                * math.factorial(degree - order_m)
                / math.factorial(degree + order_m)
            )
            if order_m > 0:
                scaling = scaling * math.sqrt(2.0)
            polar_part = scaling * legendre[degree]
            centre = degree * degree + degree
            harmonics[:, :, centre + order_m] = (
                polar_part[:, None] * np.cos(order_m * azimuth)[None, :]
            )
            if order_m > 0:
                harmonics[:, :, centre - order_m] = (
                    polar_part[:, None] * np.sin(order_m * azimuth)[None, :]
                )
    to_grid = harmonics.reshape(grid_side * grid_side, coef_count)
    quadrature = np.repeat(sine_theta * (np.pi / grid_side) * (2.0 * np.pi / grid_side), grid_side)
    from_grid = (to_grid * quadrature[:, None]).T
    return (
        jnp.asarray(to_grid, jnp.float32).astype(jnp.bfloat16),
        jnp.asarray(from_grid, jnp.float32).astype(jnp.bfloat16),
    )


def matmul_plain(left, right):
    return jnp.dot(left, right, preferred_element_type=jnp.float32)


def matmul_flip(left, right):
    return lax.dot_general(
        left, right, (((1,), (1,)), ((), ())), preferred_element_type=jnp.float32
    )


def ffn_backward(ffn_rows, grad_rows, ffn_up, ffn_down, to_grid, from_grid):
    atom_count, coef_count, channels = ffn_rows.shape
    grid_feat = jnp.einsum(
        "pk,akc->apc", to_grid, ffn_rows, preferred_element_type=jnp.float32
    ).astype(jnp.bfloat16)
    grid_points = grid_feat.shape[1]
    pre_act = matmul_plain(grid_feat.reshape(atom_count * grid_points, channels), ffn_up)
    grad_value = jnp.einsum(
        "kp,akc->apc", from_grid, grad_rows, preferred_element_type=jnp.float32
    ).astype(jnp.bfloat16)
    grad_act = matmul_flip(grad_value.reshape(atom_count * grid_points, channels), ffn_down)
    sigmoid_pre = jax.nn.sigmoid(pre_act)
    grad_pre = (grad_act * sigmoid_pre * (1.0 + pre_act * (1.0 - sigmoid_pre))).astype(jnp.bfloat16)
    grad_grid = matmul_flip(grad_pre, ffn_up).astype(jnp.bfloat16)
    ffn_term = jnp.einsum(
        "pk,apc->akc",
        to_grid,
        grad_grid.reshape(atom_count, grid_points, channels),
        preferred_element_type=jnp.float32,
    )
    return (grad_rows.astype(jnp.float32) + ffn_term).astype(jnp.bfloat16)


def so2_higher(rotated, w_one, w_two, degree_max, channels):
    cut_a = (degree_max + 1) * channels
    cut_b = cut_a + degree_max * channels
    cut_c = cut_b + degree_max * channels
    cut_d = cut_c + (degree_max - 1) * channels
    one_plus = rotated[:, cut_a:cut_b]
    one_minus = rotated[:, cut_b:cut_c]
    two_plus = rotated[:, cut_c:cut_d]
    two_minus = rotated[:, cut_d:]
    out_one_plus = matmul_plain(one_plus, w_one[0]) - matmul_plain(one_minus, w_one[1])
    out_one_minus = matmul_plain(one_minus, w_one[0]) + matmul_plain(one_plus, w_one[1])
    out_two_plus = matmul_plain(two_plus, w_two[0]) - matmul_plain(two_minus, w_two[1])
    out_two_minus = matmul_plain(two_minus, w_two[0]) + matmul_plain(two_plus, w_two[1])
    return jnp.concatenate([out_one_plus, out_one_minus, out_two_plus, out_two_minus], axis=1)


def so2_forward(rotated, weights, degree_max, channels):
    w_zero, w_one, w_two = weights
    cut_a = (degree_max + 1) * channels
    out_zero = matmul_plain(rotated[:, :cut_a], w_zero)
    return jnp.concatenate(
        [out_zero, so2_higher(rotated, w_one, w_two, degree_max, channels)], axis=1
    )


def so2_backward(grad_pre, weights, degree_max, channels):
    w_zero, w_one, w_two = weights
    cut_a = (degree_max + 2) * channels
    cut_b = cut_a + degree_max * channels
    cut_c = cut_b + degree_max * channels
    cut_d = cut_c + (degree_max - 1) * channels
    grad_zero = grad_pre[:, :cut_a]
    grad_one_plus = grad_pre[:, cut_a:cut_b]
    grad_one_minus = grad_pre[:, cut_b:cut_c]
    grad_two_plus = grad_pre[:, cut_c:cut_d]
    grad_two_minus = grad_pre[:, cut_d:]
    back_zero = matmul_flip(grad_zero, w_zero)
    back_one_plus = matmul_flip(grad_one_plus, w_one[0]) + matmul_flip(grad_one_minus, w_one[1])
    back_one_minus = matmul_flip(grad_one_minus, w_one[0]) - matmul_flip(grad_one_plus, w_one[1])
    back_two_plus = matmul_flip(grad_two_plus, w_two[0]) + matmul_flip(grad_two_minus, w_two[1])
    back_two_minus = matmul_flip(grad_two_minus, w_two[0]) - matmul_flip(grad_two_plus, w_two[1])
    return jnp.concatenate(
        [back_zero, back_one_plus, back_one_minus, back_two_plus, back_two_minus], axis=1
    )


def gate_backward(hidden, grad_o, degree_max):
    gate_index = degree_max + 1
    scalar_pre = hidden[:, 0]
    gate_pre = hidden[:, gate_index]
    sigmoid_gate = jax.nn.sigmoid(gate_pre)
    sigmoid_scalar = jax.nn.sigmoid(scalar_pre)
    grad_scalar = grad_o[:, 0] * sigmoid_scalar * (1.0 + scalar_pre * (1.0 - sigmoid_scalar))
    gated_rows = jnp.concatenate([hidden[:, 1:gate_index], hidden[:, gate_index + 1 :]], axis=1)
    grad_rows = grad_o[:, 1:]
    grad_gate = jnp.sum(grad_rows * gated_rows, axis=1) * sigmoid_gate * (1.0 - sigmoid_gate)
    grad_gated = grad_rows * sigmoid_gate[:, None, :]
    return jnp.concatenate(
        [
            grad_scalar[:, None],
            grad_gated[:, :degree_max],
            grad_gate[:, None],
            grad_gated[:, degree_max:],
        ],
        axis=1,
    )


def on_device(
    feat_in,
    ffn_in,
    grad_out,
    ffn_up,
    ffn_down,
    so2_zero,
    so2_one,
    so2_two,
    wigner,
    edge_src,
    edge_tgt,
    edge_angle,
    edge_radial,
    edge_count,
):
    atom_count, coef_count, channels = feat_in.shape
    angle_bins, kept_rows = (wigner.shape[0], wigner.shape[1])
    slot_total = edge_src.shape[2]
    block_rows = min(128, slot_total)
    to_grid, from_grid = sphere_tables(LMAX, GRID_SIDE)
    source_all = lax.all_gather(feat_in, "tgt", axis=0, tiled=True)
    source_count = source_all.shape[0]
    source_flat = source_all.reshape(source_count, coef_count * channels)
    forward_weights = (
        lax.all_gather(so2_zero, "tgt", axis=0, tiled=True),
        lax.all_gather(so2_one, "tgt", axis=1, tiled=True),
        lax.all_gather(so2_two, "tgt", axis=1, tiled=True),
    )
    target_grad = ffn_backward(ffn_in, grad_out, ffn_up, ffn_down, to_grid, from_grid)
    target_all = lax.all_gather(target_grad, "src", axis=0, tiled=True)
    target_count = target_all.shape[0]
    target_flat = target_all.reshape(target_count, coef_count * channels)
    wigner_flat = wigner.reshape(angle_bins, kept_rows * coef_count)
    src_slots = edge_src.reshape(slot_total)
    tgt_slots = edge_tgt.reshape(slot_total)
    angle_slots = edge_angle.reshape(slot_total)
    radial_slots = edge_radial.reshape(slot_total, channels)
    live_count = edge_count.reshape(())
    source_labels = jnp.arange(source_count, dtype=jnp.int32)
    target_labels = jnp.arange(target_count, dtype=jnp.int32)
    angle_labels = jnp.arange(angle_bins, dtype=jnp.int32)
    block_count = slot_total // block_rows

    def rotate_block():
        pick_source = (src_slots[:, None] == source_labels[None, :]).astype(jnp.bfloat16)
        source_rows = (
            matmul_plain(pick_source, source_flat)
            .astype(jnp.bfloat16)
            .reshape(block_rows, coef_count, channels)
        )
        pick_angle = (angle_slots[:, None] == angle_labels[None, :]).astype(jnp.bfloat16)
        rotation = (
            matmul_plain(pick_angle, wigner_flat)
            .astype(jnp.bfloat16)
            .reshape(block_rows, kept_rows, coef_count)
        )
        rotated = jnp.einsum(
            "erk,ekc->erc", rotation, source_rows, preferred_element_type=jnp.float32
        ).astype(jnp.bfloat16)
        return (rotated.reshape(block_rows, kept_rows * channels), rotation)

    def forward_step(block_index, buffers):
        first_slot = block_index * block_rows
        rotated, rotation = rotate_block()
        hidden = so2_forward(rotated, forward_weights, LMAX, channels)
        hidden = (
            hidden.reshape(block_rows, kept_rows + 1, channels)
            * radial_slots.astype(jnp.float32)[:, None, :]
        )
        hidden_all = hidden.reshape(block_rows, (kept_rows + 1) * channels)
        return (hidden_all, rotation)

    hidden_all, rotation_all = lax.fori_loop(
        0,
        block_count,
        forward_step,
        (
            jnp.zeros((slot_total, (kept_rows + 1) * channels), jnp.float32),
            jnp.zeros((slot_total, kept_rows, coef_count), jnp.bfloat16),
        ),
    )

    def backward_step(block_index, partial_value):
        first_slot = block_index * block_rows
        radial = radial_slots.astype(jnp.float32)
        pick_target = (tgt_slots[:, None] == target_labels[None, :]).astype(jnp.bfloat16)
        target_rows = (
            matmul_plain(pick_target, target_flat)
            .astype(jnp.bfloat16)
            .reshape(block_rows, coef_count, channels)
        )
        hidden = hidden_all.reshape(block_rows, kept_rows + 1, channels)
        grad_o = (
            jnp.einsum(
                "erk,ekc->erc", rotation_all, target_rows, preferred_element_type=jnp.float32
            )
            * message_scale
        )
        grad_hidden = gate_backward(hidden, grad_o, LMAX)
        grad_pre = (
            (grad_hidden * radial[:, None, :])
            .astype(jnp.bfloat16)
            .reshape(block_rows, (kept_rows + 1) * channels)
        )
        grad_rot = (
            so2_backward(grad_pre, forward_weights, LMAX, channels)
            .astype(jnp.bfloat16)
            .reshape(block_rows, kept_rows, channels)
        )
        grad_edge = jnp.einsum(
            "erk,erc->ekc", rotation_all, grad_rot, preferred_element_type=jnp.float32
        ).astype(jnp.bfloat16)
        live_slot = first_slot + jnp.arange(block_rows, dtype=jnp.int32) < live_count
        pick_back = ((src_slots[:, None] == source_labels[None, :]) & live_slot[:, None]).astype(
            jnp.bfloat16
        )
        return partial_value + lax.dot_general(
            pick_back,
            grad_edge.reshape(block_rows, coef_count * channels),
            (((0,), (0,)), ((), ())),
            preferred_element_type=jnp.float32,
        )

    partial_value = lax.fori_loop(
        0, block_count, backward_step, jnp.zeros((source_count, coef_count * channels), jnp.float32)
    )
    summed = lax.psum_scatter(
        partial_value.reshape(source_count, coef_count, channels),
        "tgt",
        scatter_dimension=0,
        tiled=True,
    )
    return (target_grad.astype(jnp.float32) + summed).astype(jnp.bfloat16)


MESH = pl.DeviceIdType.MESH
PAD = 64


def plan_fits(n_src, so2_zero, so2_one, so2_two):
    return (
        n_src == 2**3
        and so2_zero.shape[0] % 16 == 0
        and so2_zero.shape[1] % 512 == 0
        and so2_one.shape[1] % 32 == 0
        and so2_two.shape[1] % 32 == 0
    )


def mm(left, right):
    return jnp.dot(left, right, preferred_element_type=jnp.float32)


def mm_nt(left, right):
    return lax.dot_general(left, right, (((1,), (1,)), ((), ())), preferred_element_type=jnp.float32)


def sigmoid(value):
    return 1.0 / (1.0 + jnp.exp(-value))


def fused_kernel(
    n_src,
    n_tgt,
    to_grid,
    from_grid_t,
    to_grid_t,
    feat,
    ffn,
    gout,
    up,
    down,
    w0_in,
    w1_in,
    w2_in,
    wig,
    esrc,
    etgt,
    eang,
    radial,
    count,
    out,
    w0,
    w1,
    w2,
    feat_all,
    targ_all,
    part,
    recv_part,
    xs_t,
    z0,
    z1,
    z2,
    grad_o,
    hid,
    g0,
    g1,
    g2,
    wsend,
    wrecv,
    local_sem,
    fsend,
    frecv,
    tsend,
    trecv,
    psend,
    precv,
):
    i = lax.axis_index("src")
    j = lax.axis_index("tgt")
    y, x, core = i // 4, (i // 2) % 2, i % 2
    bf, f32 = jnp.bfloat16, jnp.float32
    coef, channels = feat.shape
    slots = radial.shape[0]
    angles = wig.shape[1]
    kept = wig.shape[0]
    rows0, rows1, rows2 = w0_in.shape[0], w1_in.shape[1], w2_in.shape[1]
    cols0 = w0_in.shape[1] // 4

    def chip_index(yy, xx, cc):
        return yy * 4 + xx * 2 + cc

    to_x = (chip_index(y, 1 - x, core), j)
    to_y = (chip_index(1 - y, x, core), j)
    to_core = (chip_index(y, x, 1 - core), j)
    z_peers = [(i, (j + t) % n_tgt) for t in range(1, n_tgt)]
    plane_peers = [((i + t) % n_src, j) for t in range(1, n_src)]

    barrier = pltpu.get_barrier_semaphore()
    for peer in z_peers + plane_peers:
        pl.semaphore_signal(barrier, inc=1, device_id=peer, device_id_type=MESH)

    locals_ = [
        pltpu.make_async_copy(w0_in, w0.at[pl.ds(pl.multiple_of(j * rows0, 16), rows0), :], local_sem.at[0]),
        pltpu.make_async_copy(w1_in, w1.at[:, pl.ds(pl.multiple_of(j * rows1, 16), rows1), :], local_sem.at[1]),
        pltpu.make_async_copy(w2_in, w2.at[:, pl.ds(pl.multiple_of(j * rows2, 16), rows2), :], local_sem.at[2]),
    ]
    for copy in locals_:
        copy.start()

    spread = (
        lax.broadcasted_iota(jnp.int32, (PAD, coef), 0) == lax.broadcasted_iota(jnp.int32, (PAD, coef), 1)
    ).astype(bf)
    feat_all[pl.ds(pl.multiple_of(j * PAD, PAD), PAD), :] = mm(spread, feat[...]).astype(bf)

    pl.semaphore_wait(barrier, len(z_peers) + len(plane_peers))

    def remote(source, target, send, recv, peer):
        return pltpu.make_async_remote_copy(
            src_ref=source, dst_ref=target, send_sem=send, recv_sem=recv, device_id=peer, device_id_type=MESH
        )

    def piece(c, shard, yy, xx):
        if c == 0:
            half = rows1 // 2
            return [w1.at[yy, pl.ds(pl.multiple_of(shard * rows1 + xx * half, 16), half), :]]
        half = rows2 // 2
        return [
            w0.at[
                pl.ds(pl.multiple_of(shard * rows0, 16), rows0),
                pl.ds(pl.multiple_of((yy * 2 + xx) * cols0, 128), cols0),
            ],
            w2.at[yy, pl.ds(pl.multiple_of(shard * rows2 + xx * half, 16), half), :],
        ]

    def own_piece(c):
        if c == 0:
            half = rows1 // 2
            return [w1_in.at[y, pl.ds(pl.multiple_of(x * half, 16), half), :]]
        half = rows2 // 2
        return [
            w0_in.at[:, pl.ds(pl.multiple_of((y * 2 + x) * cols0, 128), cols0)],
            w2_in.at[y, pl.ds(pl.multiple_of(x * half, 16), half), :],
        ]

    def origin(o):
        return (1 - y if o >= 2 else y, 1 - x if o % 2 else x)

    def piece_from(c, t, o):
        yy, xx = origin(o)
        return piece(c, (j + n_tgt - t) % n_tgt, yy, xx)

    def start_z(c):
        for t in range(1, n_tgt):
            for a, (source, target) in enumerate(zip(own_piece(c), piece(c, j, y, x))):
                remote(source, target, wsend.at[t - 1, 0, a], wrecv.at[0, t - 1, 0, a], z_peers[t - 1]).start()

    def send(c, t, o, slot, kind, to_o, peer):
        for a, ref in enumerate(piece_from(c, t, o)):
            remote(ref, ref, wsend.at[t - 1, slot, a], wrecv.at[kind, t - 1, to_o, a], peer).start()

    def arrive(c, t, o, kind):
        for a, ref in enumerate(piece_from(c, t, o)):
            remote(ref, ref, wsend.at[t - 1, 0, a], wrecv.at[kind, t - 1, o, a], to_core).wait_recv()

    def relay_own(c, t):
        arrive(c, t, 0, 0)
        send(c, t, 0, 1, 0, 1, to_x)
        send(c, t, 0, 2, 0, 2, to_y)
        send(c, t, 0, 4, 1, 0, to_core)

    def relay(c, t):
        arrive(c, t, 1, 0)
        if c == 0:
            send(c, t, 1, 3, 0, 3, to_y)
        send(c, t, 1, 5, 1, 1, to_core)
        arrive(c, t, 2, 0)
        if c == 1:
            send(c, t, 2, 3, 0, 3, to_x)
        send(c, t, 2, 6, 1, 2, to_core)

    def relay_diag(c, t):
        arrive(c, t, 3, 0)
        send(c, t, 3, 7, 1, 3, to_core)

    def finish(c):
        for t in order:
            for o in range(4):
                arrive(1 - c, t, o, 1)

    def drain(c):
        for t in range(1, n_tgt):
            for slot in range(8):
                for a, ref in enumerate(piece_from(c, t, 0)):
                    remote(ref, ref, wsend.at[t - 1, slot, a], wrecv.at[0, t - 1, 0, a], to_core).wait_send()

    def by_core(function, *args):
        for c in range(2):
            pl.when(core == c)(functools.partial(function, c, *args))

    order = [1, n_tgt - 1] + list(range(2, n_tgt - 1))
    feat_own = feat_all.at[pl.ds(pl.multiple_of(j * PAD, PAD), PAD), :]
    feat_sends = [
        remote(feat_own, feat_own, fsend.at[t - 1], frecv.at[t - 1], z_peers[t - 1]) for t in range(1, n_tgt)
    ]
    for copy in feat_sends:
        copy.start()
    by_core(start_z)

    grid_in = mm(to_grid[...], ffn[...]).astype(bf)
    pre = mm(grid_in, up[...])
    value = mm(from_grid_t[...], gout[...]).astype(bf)
    grad_act = mm_nt(value, down[...])
    sig = sigmoid(pre)
    grad_pre = (grad_act * sig * (1.0 + pre * (1.0 - sig))).astype(bf)
    grad_grid = mm_nt(grad_pre, up[...]).astype(bf)
    target = (mm(spread, gout[...]) + mm(to_grid_t[...], grad_grid)).astype(bf)
    targ_all[pl.ds(pl.multiple_of(i * PAD, PAD), PAD), :] = target
    targ_own = targ_all.at[pl.ds(pl.multiple_of(i * PAD, PAD), PAD), :]
    targ_sends = [
        remote(targ_own, targ_own, tsend.at[t - 1], trecv.at[t - 1], plane_peers[t - 1]) for t in range(1, n_src)
    ]
    for copy in targ_sends:
        copy.start()

    by_core(relay_own, order[0])

    def iota(shape, axis):
        return lax.broadcasted_iota(jnp.int32, shape, axis)

    eye = (iota((slots, slots), 0) == iota((slots, slots), 1)).astype(bf)
    pick_angle_t = (iota((angles, slots), 0) == eang[...]).astype(bf)
    n_s, n_t = n_tgt * PAD, n_src * PAD
    live = iota((1, slots), 1) < count[...]
    mask_s_t = ((iota((n_s, slots), 0) // PAD == esrc[...]) & live).astype(bf)
    mask_t_t = (iota((n_t, slots), 0) // PAD == etgt[...]).astype(bf)
    pick_angle = mm_nt(eye, pick_angle_t).astype(bf)
    mask_s = mm_nt(eye, mask_s_t).astype(bf)
    mask_t = mm_nt(eye, mask_t_t).astype(bf)
    spread_s = (iota((coef, n_s), 1) % PAD == iota((coef, n_s), 0)).astype(bf)
    spread_t = (iota((coef, n_t), 1) % PAD == iota((coef, n_t), 0)).astype(bf)
    spread_s_t = (iota((n_s, coef), 0) % PAD == iota((n_s, coef), 1)).astype(bf)

    by_core(relay_own, order[1])
    for r in range(kept):
        wide = mm_nt(spread_s_t, wig[r]).astype(bf)
        xs_t[:, r * slots : (r + 1) * slots] = mm(wide, pick_angle_t).astype(bf) * mask_s_t
    for t in range(2, n_tgt - 1):
        by_core(relay_own, t)

    for copy in feat_sends:
        copy.wait_recv()
    feats = feat_all[...]
    degree_cut = [7, 13, 19, 24, 29]
    for r in range(kept):
        turn = mm(mm(pick_angle, wig[r]).astype(bf), spread_s).astype(bf) * mask_s
        row = mm(turn, feats).astype(bf)
        if r < degree_cut[0]:
            z0[:, r * channels : (r + 1) * channels] = row
        elif r < degree_cut[2]:
            p, at = divmod(r - degree_cut[0], 6)
            z1[p * slots : (p + 1) * slots, at * channels : (at + 1) * channels] = row
        else:
            p, at = divmod(r - degree_cut[2], 5)
            z2[p * slots : (p + 1) * slots, at * channels : (at + 1) * channels] = row
    by_core(relay, order[0])

    for copy in targ_sends:
        copy.wait_recv()
    targets = targ_all[...]
    for r in range(kept):
        turn = mm(mm(pick_angle, wig[r]).astype(bf), spread_t).astype(bf) * mask_t
        grad_o[r] = mm(turn, targets) * message_scale
        if r == 9:
            by_core(relay, order[1])
        if r == 19:
            by_core(relay_diag, order[0])
    for t in range(2, n_tgt - 1):
        by_core(relay, t)
    by_core(relay_diag, order[1])
    for t in range(2, n_tgt - 1):
        by_core(relay_diag, t)
    for copy in locals_:
        copy.wait()
    by_core(finish)

    gain = radial[...].astype(f32)
    h0 = mm(z0[...], w0[...])
    for r in range(8):
        hid[r] = h0[:, r * channels : (r + 1) * channels] * gain
    for first, per, zz, ww in ((8, 6, z1, w1), (20, 5, z2, w2)):
        real = mm(zz[...], ww[0])
        imag = mm(zz[...], ww[1])
        plus = real[:slots] - imag[slots:]
        minus = real[slots:] + imag[:slots]
        for r in range(per):
            cut = slice(r * channels, (r + 1) * channels)
            hid[first + r] = plus[:, cut] * gain
            hid[first + per + r] = minus[:, cut] * gain

    sig_gate = sigmoid(hid[7])
    scalar = hid[0]
    sig_scalar = sigmoid(scalar)
    g0[:, :channels] = (grad_o[0] * sig_scalar * (1.0 + scalar * (1.0 - sig_scalar)) * gain).astype(bf)
    gate_gain = sig_gate * gain
    total = jnp.zeros((slots, channels), f32)
    for r in range(1, kept):
        row = grad_o[r]
        total = total + row * hid[r if r < 7 else r + 1]
        value_r = (row * gate_gain).astype(bf)
        if r < 7:
            g0[:, r * channels : (r + 1) * channels] = value_r
        elif r < 19:
            p, at = divmod(r - 7, 6)
            g1[p * slots : (p + 1) * slots, at * channels : (at + 1) * channels] = value_r
        else:
            p, at = divmod(r - 19, 5)
            g2[p * slots : (p + 1) * slots, at * channels : (at + 1) * channels] = value_r
    g0[:, 7 * channels :] = (total * sig_gate * (1.0 - sig_gate) * gain).astype(bf)

    back = mm_nt(g0[...], w0[...]).astype(bf)
    rows = [back[:, r * channels : (r + 1) * channels] for r in range(7)]
    for per, gg, ww in ((6, g1, w1), (5, g2, w2)):
        real = mm_nt(gg[...], ww[0])
        imag = mm_nt(gg[...], ww[1])
        plus = (real[:slots] + imag[slots:]).astype(bf)
        minus = (real[slots:] - imag[:slots]).astype(bf)
        rows += [plus[:, r * channels : (r + 1) * channels] for r in range(per)]
        rows += [minus[:, r * channels : (r + 1) * channels] for r in range(per)]
    part[...] = mm(xs_t[...], jnp.concatenate(rows, axis=0))

    part_sends = [
        remote(
            part.at[pl.ds(pl.multiple_of(((j + t) % n_tgt) * PAD, PAD), PAD), :],
            recv_part.at[t - 1],
            psend.at[t - 1],
            precv.at[t - 1],
            z_peers[t - 1],
        )
        for t in range(1, n_tgt)
    ]
    for copy in part_sends:
        copy.start()
    by_core(drain)
    for copy in feat_sends + targ_sends:
        copy.wait_send()
    summed = part[pl.ds(pl.multiple_of(j * PAD, PAD), PAD), :]
    for t, copy in enumerate(part_sends):
        copy.wait_recv()
        summed = summed + recv_part[t]
    mine = targ_all[pl.ds(pl.multiple_of(i * PAD, PAD), PAD), :].astype(f32)
    out[...] = (mine + summed)[:coef].astype(bf)
    for copy in part_sends:
        copy.wait_send()


def fused_on_device(
    feat_in,
    ffn_in,
    grad_out,
    ffn_up,
    ffn_down,
    so2_zero,
    so2_one,
    so2_two,
    wigner,
    edge_src,
    edge_tgt,
    edge_angle,
    edge_radial,
    edge_count,
):
    n_src, n_tgt = lax.axis_size("src"), lax.axis_size("tgt")
    _, coef, channels = feat_in.shape
    kept = wigner.shape[1]
    slots = edge_src.shape[2]
    to_grid, from_grid = sphere_tables(LMAX, GRID_SIDE)
    more = -to_grid.shape[0] % 16
    to_grid = jnp.pad(to_grid, ((0, more), (0, 0)))
    from_grid_t = jnp.pad(from_grid.T, ((0, more), (0, 0)))
    to_grid_t = jnp.pad(to_grid.T, ((0, PAD - coef), (0, 0)))
    bf, f32 = jnp.bfloat16, jnp.float32
    k0, k1, k2 = so2_zero.shape[0] * n_tgt, so2_one.shape[1] * n_tgt, so2_two.shape[1] * n_tgt
    vmem = pl.BlockSpec(memory_space=pltpu.VMEM)
    hbm = pl.BlockSpec(memory_space=pl.ANY)
    dma = pltpu.SemaphoreType.DMA
    result = pl.pallas_call(
        functools.partial(fused_kernel, n_src, n_tgt),
        out_shape=jax.ShapeDtypeStruct((coef, channels), bf),
        in_specs=[vmem] * 8 + [hbm] * 3 + [vmem] * 6,
        out_specs=vmem,
        scratch_shapes=[
            pltpu.VMEM((k0, so2_zero.shape[1]), bf),
            pltpu.VMEM((2, k1, so2_one.shape[2]), bf),
            pltpu.VMEM((2, k2, so2_two.shape[2]), bf),
            pltpu.VMEM((n_tgt * PAD, channels), bf),
            pltpu.VMEM((n_src * PAD, channels), bf),
            pltpu.VMEM((n_tgt * PAD, channels), f32),
            pltpu.VMEM((n_tgt - 1, PAD, channels), f32),
            pltpu.VMEM((n_tgt * PAD, kept * slots), bf),
            pltpu.VMEM((slots, k0), bf),
            pltpu.VMEM((2 * slots, k1), bf),
            pltpu.VMEM((2 * slots, k2), bf),
            pltpu.VMEM((kept, slots, channels), f32),
            pltpu.VMEM((kept + 1, slots, channels), f32),
            pltpu.VMEM((slots, so2_zero.shape[1]), bf),
            pltpu.VMEM((2 * slots, k1), bf),
            pltpu.VMEM((2 * slots, k2), bf),
            dma((n_tgt - 1, 8, 2)),
            dma((2, n_tgt - 1, 4, 2)),
            dma((3,)),
            dma((n_tgt - 1,)),
            dma((n_tgt - 1,)),
            dma((n_src - 1,)),
            dma((n_src - 1,)),
            dma((n_tgt - 1,)),
            dma((n_tgt - 1,)),
        ],
        compiler_params=pltpu.CompilerParams(
            collective_id=0, has_side_effects=True, vmem_limit_bytes=48 * 1024 * 1024
        ),
    )(
        to_grid,
        from_grid_t,
        to_grid_t,
        feat_in.reshape(coef, channels),
        ffn_in.reshape(coef, channels),
        grad_out.reshape(coef, channels),
        ffn_up,
        ffn_down,
        so2_zero,
        so2_one,
        so2_two,
        wigner.transpose(1, 0, 2),
        edge_src.reshape(1, slots),
        edge_tgt.reshape(1, slots),
        edge_angle.reshape(1, slots),
        edge_radial.reshape(slots, channels),
        edge_count,
    )
    return result.reshape(feat_in.shape)


def choose(*args):
    if plan_fits(lax.axis_size("src"), *args[5:8]):
        return fused_on_device(*args)
    return on_device(*args)


def solution(mesh):
    placed = (
        P(("src", "tgt"), None, None),
        P(("src", "tgt"), None, None),
        P(("src", "tgt"), None, None),
        P(),
        P(),
        P("tgt", None),
        P(None, "tgt", None),
        P(None, "tgt", None),
        P(),
        P("src", "tgt", None),
        P("src", "tgt", None),
        P("src", "tgt", None),
        P("src", "tgt", None, None),
        P("src", "tgt"),
    )
    return jax.shard_map(
        choose,
        mesh=mesh,
        in_specs=placed,
        out_specs=P(("src", "tgt"), None, None),
        check_vma=False,
    )
```

```python
import functools
import math

import jax
import jax.numpy as jnp
import numpy as np
from jax import lax
from jax.experimental import pallas as pl
from jax.experimental.pallas import tpu as pltpu
from jax.sharding import PartitionSpec as P

LMAX = 6
GRID_SIDE = 14


message_scale = 0.125


def sphere_tables(degree_max, grid_side):
    polar_angle = (np.arange(grid_side) + 0.5) * np.pi / grid_side
    azimuth = np.arange(grid_side) * 2.0 * np.pi / grid_side
    cosine = np.cos(polar_angle)
    sine_theta = np.sin(polar_angle)
    coef_count = (degree_max + 1) * (degree_max + 1)
    harmonics = np.zeros((grid_side, grid_side, coef_count))
    for order_m in range(degree_max + 1):
        diagonal = np.ones(grid_side)
        for factor in range(1, order_m + 1):
            diagonal = diagonal * (2 * factor - 1) * sine_theta
        legendre = {order_m: diagonal}
        if order_m + 1 <= degree_max:
            legendre[order_m + 1] = cosine * (2 * order_m + 1) * diagonal
        for degree in range(order_m + 2, degree_max + 1):
            legendre[degree] = (
                (2 * degree - 1) * cosine * legendre[degree - 1]
                - (degree + order_m - 1) * legendre[degree - 2]
            ) / (degree - order_m)
        for degree in range(order_m, degree_max + 1):
            scaling = math.sqrt(
                (2 * degree + 1)
                / (4.0 * math.pi)
                * math.factorial(degree - order_m)
                / math.factorial(degree + order_m)
            )
            if order_m > 0:
                scaling = scaling * math.sqrt(2.0)
            polar_part = scaling * legendre[degree]
            centre = degree * degree + degree
            harmonics[:, :, centre + order_m] = (
                polar_part[:, None] * np.cos(order_m * azimuth)[None, :]
            )
            if order_m > 0:
                harmonics[:, :, centre - order_m] = (
                    polar_part[:, None] * np.sin(order_m * azimuth)[None, :]
                )
    to_grid = harmonics.reshape(grid_side * grid_side, coef_count)
    quadrature = np.repeat(sine_theta * (np.pi / grid_side) * (2.0 * np.pi / grid_side), grid_side)
    from_grid = (to_grid * quadrature[:, None]).T
    return (
        jnp.asarray(to_grid, jnp.float32).astype(jnp.bfloat16),
        jnp.asarray(from_grid, jnp.float32).astype(jnp.bfloat16),
    )


def matmul_plain(left, right):
    return jnp.dot(left, right, preferred_element_type=jnp.float32)


def matmul_flip(left, right):
    return lax.dot_general(
        left, right, (((1,), (1,)), ((), ())), preferred_element_type=jnp.float32
    )


def ffn_backward(ffn_rows, grad_rows, ffn_up, ffn_down, to_grid, from_grid):
    atom_count, coef_count, channels = ffn_rows.shape
    grid_feat = jnp.einsum(
        "pk,akc->apc", to_grid, ffn_rows, preferred_element_type=jnp.float32
    ).astype(jnp.bfloat16)
    grid_points = grid_feat.shape[1]
    pre_act = matmul_plain(grid_feat.reshape(atom_count * grid_points, channels), ffn_up)
    grad_value = jnp.einsum(
        "kp,akc->apc", from_grid, grad_rows, preferred_element_type=jnp.float32
    ).astype(jnp.bfloat16)
    grad_act = matmul_flip(grad_value.reshape(atom_count * grid_points, channels), ffn_down)
    sigmoid_pre = jax.nn.sigmoid(pre_act)
    grad_pre = (grad_act * sigmoid_pre * (1.0 + pre_act * (1.0 - sigmoid_pre))).astype(jnp.bfloat16)
    grad_grid = matmul_flip(grad_pre, ffn_up).astype(jnp.bfloat16)
    ffn_term = jnp.einsum(
        "pk,apc->akc",
        to_grid,
        grad_grid.reshape(atom_count, grid_points, channels),
        preferred_element_type=jnp.float32,
    )
    return (grad_rows.astype(jnp.float32) + ffn_term).astype(jnp.bfloat16)


def so2_higher(rotated, w_one, w_two, degree_max, channels):
    cut_a = (degree_max + 1) * channels
    cut_b = cut_a + degree_max * channels
    cut_c = cut_b + degree_max * channels
    cut_d = cut_c + (degree_max - 1) * channels
    one_plus = rotated[:, cut_a:cut_b]
    one_minus = rotated[:, cut_b:cut_c]
    two_plus = rotated[:, cut_c:cut_d]
    two_minus = rotated[:, cut_d:]
    out_one_plus = matmul_plain(one_plus, w_one[0]) - matmul_plain(one_minus, w_one[1])
    out_one_minus = matmul_plain(one_minus, w_one[0]) + matmul_plain(one_plus, w_one[1])
    out_two_plus = matmul_plain(two_plus, w_two[0]) - matmul_plain(two_minus, w_two[1])
    out_two_minus = matmul_plain(two_minus, w_two[0]) + matmul_plain(two_plus, w_two[1])
    return jnp.concatenate([out_one_plus, out_one_minus, out_two_plus, out_two_minus], axis=1)


def so2_forward(rotated, weights, degree_max, channels):
    w_zero, w_one, w_two = weights
    cut_a = (degree_max + 1) * channels
    out_zero = matmul_plain(rotated[:, :cut_a], w_zero)
    return jnp.concatenate(
        [out_zero, so2_higher(rotated, w_one, w_two, degree_max, channels)], axis=1
    )


def so2_backward(grad_pre, weights, degree_max, channels):
    w_zero, w_one, w_two = weights
    cut_a = (degree_max + 2) * channels
    cut_b = cut_a + degree_max * channels
    cut_c = cut_b + degree_max * channels
    cut_d = cut_c + (degree_max - 1) * channels
    grad_zero = grad_pre[:, :cut_a]
    grad_one_plus = grad_pre[:, cut_a:cut_b]
    grad_one_minus = grad_pre[:, cut_b:cut_c]
    grad_two_plus = grad_pre[:, cut_c:cut_d]
    grad_two_minus = grad_pre[:, cut_d:]
    back_zero = matmul_flip(grad_zero, w_zero)
    back_one_plus = matmul_flip(grad_one_plus, w_one[0]) + matmul_flip(grad_one_minus, w_one[1])
    back_one_minus = matmul_flip(grad_one_minus, w_one[0]) - matmul_flip(grad_one_plus, w_one[1])
    back_two_plus = matmul_flip(grad_two_plus, w_two[0]) + matmul_flip(grad_two_minus, w_two[1])
    back_two_minus = matmul_flip(grad_two_minus, w_two[0]) - matmul_flip(grad_two_plus, w_two[1])
    return jnp.concatenate(
        [back_zero, back_one_plus, back_one_minus, back_two_plus, back_two_minus], axis=1
    )


def gate_backward(hidden, grad_o, degree_max):
    gate_index = degree_max + 1
    scalar_pre = hidden[:, 0]
    gate_pre = hidden[:, gate_index]
    sigmoid_gate = jax.nn.sigmoid(gate_pre)
    sigmoid_scalar = jax.nn.sigmoid(scalar_pre)
    grad_scalar = grad_o[:, 0] * sigmoid_scalar * (1.0 + scalar_pre * (1.0 - sigmoid_scalar))
    gated_rows = jnp.concatenate([hidden[:, 1:gate_index], hidden[:, gate_index + 1 :]], axis=1)
    grad_rows = grad_o[:, 1:]
    grad_gate = jnp.sum(grad_rows * gated_rows, axis=1) * sigmoid_gate * (1.0 - sigmoid_gate)
    grad_gated = grad_rows * sigmoid_gate[:, None, :]
    return jnp.concatenate(
        [
            grad_scalar[:, None],
            grad_gated[:, :degree_max],
            grad_gate[:, None],
            grad_gated[:, degree_max:],
        ],
        axis=1,
    )


def on_device(
    feat_in,
    ffn_in,
    grad_out,
    ffn_up,
    ffn_down,
    so2_zero,
    so2_one,
    so2_two,
    wigner,
    edge_src,
    edge_tgt,
    edge_angle,
    edge_radial,
    edge_count,
):
    atom_count, coef_count, channels = feat_in.shape
    angle_bins, kept_rows = (wigner.shape[0], wigner.shape[1])
    slot_total = edge_src.shape[2]
    block_rows = min(128, slot_total)
    to_grid, from_grid = sphere_tables(LMAX, GRID_SIDE)
    source_all = lax.all_gather(feat_in, "tgt", axis=0, tiled=True)
    source_count = source_all.shape[0]
    source_flat = source_all.reshape(source_count, coef_count * channels)
    forward_weights = (
        lax.all_gather(so2_zero, "tgt", axis=0, tiled=True),
        lax.all_gather(so2_one, "tgt", axis=1, tiled=True),
        lax.all_gather(so2_two, "tgt", axis=1, tiled=True),
    )
    target_grad = ffn_backward(ffn_in, grad_out, ffn_up, ffn_down, to_grid, from_grid)
    target_all = lax.all_gather(target_grad, "src", axis=0, tiled=True)
    target_count = target_all.shape[0]
    target_flat = target_all.reshape(target_count, coef_count * channels)
    wigner_flat = wigner.reshape(angle_bins, kept_rows * coef_count)
    src_slots = edge_src.reshape(slot_total)
    tgt_slots = edge_tgt.reshape(slot_total)
    angle_slots = edge_angle.reshape(slot_total)
    radial_slots = edge_radial.reshape(slot_total, channels)
    live_count = edge_count.reshape(())
    source_labels = jnp.arange(source_count, dtype=jnp.int32)
    target_labels = jnp.arange(target_count, dtype=jnp.int32)
    angle_labels = jnp.arange(angle_bins, dtype=jnp.int32)
    block_count = slot_total // block_rows

    def rotate_block():
        pick_source = (src_slots[:, None] == source_labels[None, :]).astype(jnp.bfloat16)
        source_rows = (
            matmul_plain(pick_source, source_flat)
            .astype(jnp.bfloat16)
            .reshape(block_rows, coef_count, channels)
        )
        pick_angle = (angle_slots[:, None] == angle_labels[None, :]).astype(jnp.bfloat16)
        rotation = (
            matmul_plain(pick_angle, wigner_flat)
            .astype(jnp.bfloat16)
            .reshape(block_rows, kept_rows, coef_count)
        )
        rotated = jnp.einsum(
            "erk,ekc->erc", rotation, source_rows, preferred_element_type=jnp.float32
        ).astype(jnp.bfloat16)
        return (rotated.reshape(block_rows, kept_rows * channels), rotation)

    def forward_step(block_index, buffers):
        first_slot = block_index * block_rows
        rotated, rotation = rotate_block()
        hidden = so2_forward(rotated, forward_weights, LMAX, channels)
        hidden = (
            hidden.reshape(block_rows, kept_rows + 1, channels)
            * radial_slots.astype(jnp.float32)[:, None, :]
        )
        hidden_all = hidden.reshape(block_rows, (kept_rows + 1) * channels)
        return (hidden_all, rotation)

    hidden_all, rotation_all = lax.fori_loop(
        0,
        block_count,
        forward_step,
        (
            jnp.zeros((slot_total, (kept_rows + 1) * channels), jnp.float32),
            jnp.zeros((slot_total, kept_rows, coef_count), jnp.bfloat16),
        ),
    )

    def backward_step(block_index, partial_value):
        first_slot = block_index * block_rows
        radial = radial_slots.astype(jnp.float32)
        pick_target = (tgt_slots[:, None] == target_labels[None, :]).astype(jnp.bfloat16)
        target_rows = (
            matmul_plain(pick_target, target_flat)
            .astype(jnp.bfloat16)
            .reshape(block_rows, coef_count, channels)
        )
        hidden = hidden_all.reshape(block_rows, kept_rows + 1, channels)
        grad_o = (
            jnp.einsum(
                "erk,ekc->erc", rotation_all, target_rows, preferred_element_type=jnp.float32
            )
            * message_scale
        )
        grad_hidden = gate_backward(hidden, grad_o, LMAX)
        grad_pre = (
            (grad_hidden * radial[:, None, :])
            .astype(jnp.bfloat16)
            .reshape(block_rows, (kept_rows + 1) * channels)
        )
        grad_rot = (
            so2_backward(grad_pre, forward_weights, LMAX, channels)
            .astype(jnp.bfloat16)
            .reshape(block_rows, kept_rows, channels)
        )
        grad_edge = jnp.einsum(
            "erk,erc->ekc", rotation_all, grad_rot, preferred_element_type=jnp.float32
        ).astype(jnp.bfloat16)
        live_slot = first_slot + jnp.arange(block_rows, dtype=jnp.int32) < live_count
        pick_back = ((src_slots[:, None] == source_labels[None, :]) & live_slot[:, None]).astype(
            jnp.bfloat16
        )
        return partial_value + lax.dot_general(
            pick_back,
            grad_edge.reshape(block_rows, coef_count * channels),
            (((0,), (0,)), ((), ())),
            preferred_element_type=jnp.float32,
        )

    partial_value = lax.fori_loop(
        0, block_count, backward_step, jnp.zeros((source_count, coef_count * channels), jnp.float32)
    )
    summed = lax.psum_scatter(
        partial_value.reshape(source_count, coef_count, channels),
        "tgt",
        scatter_dimension=0,
        tiled=True,
    )
    return (target_grad.astype(jnp.float32) + summed).astype(jnp.bfloat16)


MESH = pl.DeviceIdType.MESH
PAD = 64


def plan_fits(n_src, n_tgt, so2_zero, so2_one, so2_two):
    return (
        n_src == 2**3
        and n_tgt == 2**2
        and so2_zero.shape[0] % 16 == 0
        and so2_zero.shape[1] % 512 == 0
        and so2_one.shape[1] % 32 == 0
        and so2_two.shape[1] % 32 == 0
    )


def mm(left, right):
    return jnp.dot(left, right, preferred_element_type=jnp.float32)


def mm_nt(left, right):
    return lax.dot_general(left, right, (((1,), (1,)), ((), ())), preferred_element_type=jnp.float32)


def sigmoid(value):
    return 1.0 / (1.0 + jnp.exp(-value))


def fused_kernel(
    n_src,
    n_tgt,
    to_grid_in,
    from_grid_t_in,
    to_grid_t_in,
    feat_in,
    ffn_in,
    gout_in,
    up_in,
    down_in,
    w0_in,
    w1_in,
    w2_in,
    wig_in,
    esrc_in,
    etgt_in,
    eang_in,
    radial_in,
    count,
    out,
    to_grid,
    from_grid_t,
    to_grid_t,
    feat,
    ffn,
    gout,
    up,
    down,
    wig,
    esrc,
    etgt,
    eang,
    radial,
    in_sem,
    w0,
    w1,
    w2,
    feat_all,
    targ_all,
    part,
    recv_part,
    table_s,
    table_t,
    xs_t,
    z0,
    z1,
    z2,
    grad_o,
    hid,
    g0,
    g1,
    g2,
    osend,
    wsend,
    wrecv,
    local_sem,
    fsend,
    frecv,
    tsend,
    trecv,
    psend,
    precv,
):
    i = lax.axis_index("src")
    j = lax.axis_index("tgt")
    y, x, core = i // 4, (i // 2) % 2, i % 2
    bf, f32 = jnp.bfloat16, jnp.float32
    coef, channels = feat.shape
    slots = radial.shape[0]
    angles = wig.shape[1]
    kept = wig.shape[0]
    rows0, rows1, rows2 = w0_in.shape[0], w1_in.shape[1], w2_in.shape[1]
    cols0 = w0_in.shape[1] // 4

    def chip_index(yy, xx, cc):
        return yy * 4 + xx * 2 + cc

    to_x = (chip_index(y, 1 - x, core), j)
    to_y = (chip_index(1 - y, x, core), j)
    to_core = (chip_index(y, x, 1 - core), j)
    z_peers = [(i, (j + t) % n_tgt) for t in range(1, n_tgt)]
    plane_peers = [((i + t) % n_src, j) for t in range(1, n_src)]

    staged = {}
    for at, (name, source, target) in enumerate((
        ("feat", feat_in, feat),
        ("ffn", ffn_in, ffn),
        ("gout", gout_in, gout),
        ("to_grid", to_grid_in, to_grid),
        ("from_grid_t", from_grid_t_in, from_grid_t),
        ("up", up_in, up),
        ("down", down_in, down),
        ("to_grid_t", to_grid_t_in, to_grid_t),
        ("esrc", esrc_in, esrc),
        ("etgt", etgt_in, etgt),
        ("eang", eang_in, eang),
        ("wig", wig_in, wig),
        ("radial", radial_in, radial),
    )):
        staged[name] = pltpu.make_async_copy(source, target, in_sem.at[at])
        staged[name].start()

    barrier = pltpu.get_barrier_semaphore()
    for peer in z_peers + plane_peers:
        pl.semaphore_signal(barrier, inc=1, device_id=peer, device_id_type=MESH)

    locals_ = [
        pltpu.make_async_copy(w0_in, w0.at[pl.ds(pl.multiple_of(j * rows0, 16), rows0), :], local_sem.at[0]),
        pltpu.make_async_copy(w1_in, w1.at[:, pl.ds(pl.multiple_of(j * rows1, 16), rows1), :], local_sem.at[1]),
        pltpu.make_async_copy(w2_in, w2.at[:, pl.ds(pl.multiple_of(j * rows2, 16), rows2), :], local_sem.at[2]),
    ]
    for copy in locals_:
        copy.start()

    spread = (
        lax.broadcasted_iota(jnp.int32, (PAD, coef), 0) == lax.broadcasted_iota(jnp.int32, (PAD, coef), 1)
    ).astype(bf)
    staged["feat"].wait()
    feat_all[pl.ds(pl.multiple_of(j * PAD, PAD), PAD), :] = mm(spread, feat[...]).astype(bf)

    pl.semaphore_wait(barrier, len(z_peers) + len(plane_peers))

    def remote(source, target, send, recv, peer):
        return pltpu.make_async_remote_copy(
            src_ref=source, dst_ref=target, send_sem=send, recv_sem=recv, device_id=peer, device_id_type=MESH
        )

    def piece(c, shard, yy, xx):
        if c == 0:
            half = rows1 // 2
            return [w1.at[yy, pl.ds(pl.multiple_of(shard * rows1 + xx * half, 16), half), :]]
        half = rows2 // 2
        return [
            w0.at[
                pl.ds(pl.multiple_of(shard * rows0, 16), rows0),
                pl.ds(pl.multiple_of((yy * 2 + xx) * cols0, 128), cols0),
            ],
            w2.at[yy, pl.ds(pl.multiple_of(shard * rows2 + xx * half, 16), half), :],
        ]

    def own_piece(c):
        if c == 0:
            half = rows1 // 2
            return [w1_in.at[y, pl.ds(pl.multiple_of(x * half, 16), half), :]]
        half = rows2 // 2
        return [
            w0_in.at[:, pl.ds(pl.multiple_of((y * 2 + x) * cols0, 128), cols0)],
            w2_in.at[y, pl.ds(pl.multiple_of(x * half, 16), half), :],
        ]

    def origin(o):
        return (1 - y if o >= 2 else y, 1 - x if o % 2 else x)

    def piece_from(c, t, o):
        yy, xx = origin(o)
        return piece(c, (j + n_tgt - t) % n_tgt, yy, xx)

    last = n_tgt - 1
    lowest, highest = (last - j) // last, j // last
    t_first = 1 + 2 * lowest
    t_third = 2 - lowest + highest
    order = [t_first, 6 - t_first - t_third, t_third]
    above, below = (i, (j + 1) % n_tgt), (i, (j + n_tgt - 1) % n_tgt)

    def own_copies(c, up_way):
        t, peer = (1, above) if up_way else (last, below)
        return [
            remote(source, target, osend.at[int(up_way), a], wrecv.at[0, t - 1, 0, a], peer)
            for a, (source, target) in enumerate(zip(own_piece(c), piece(c, j, y, x)))
        ]

    def start_z(c):
        @pl.when(j < last)
        def _():
            for copy in own_copies(c, True):
                copy.start()

        @pl.when(j > 0)
        def _():
            for copy in own_copies(c, False):
                copy.start()

    def send(c, t, o, slot, kind, to_o, peer):
        for a, ref in enumerate(piece_from(c, t, o)):
            remote(ref, ref, wsend.at[t - 1, slot, a], wrecv.at[kind, t - 1, to_o, a], peer).start()

    def onward(c, t, to_t, peer):
        for a, ref in enumerate(piece_from(c, t, 0)):
            remote(ref, ref, wsend.at[t - 1, 0, a], wrecv.at[0, to_t - 1, 0, a], peer).start()

    def arrive(c, t, o, kind):
        for a, ref in enumerate(piece_from(c, t, o)):
            remote(ref, ref, wsend.at[t - 1, 0, a], wrecv.at[kind, t - 1, o, a], to_core).wait_recv()

    def relay_own(c, t):
        arrive(c, t, 0, 0)

        @pl.when((t <= j) & (j < last))
        def _():
            onward(c, t, t + 1, above)

        @pl.when((t > j) & (j > 0))
        def _():
            onward(c, t, t - 1, below)

        send(c, t, 0, 1, 0, 1, to_x)
        send(c, t, 0, 2, 0, 2, to_y)
        send(c, t, 0, 4, 1, 0, to_core)

    def relay(c, t):
        arrive(c, t, 1, 0)
        if c == 0:
            send(c, t, 1, 3, 0, 3, to_y)
        send(c, t, 1, 5, 1, 1, to_core)
        arrive(c, t, 2, 0)
        if c == 1:
            send(c, t, 2, 3, 0, 3, to_x)
        send(c, t, 2, 6, 1, 2, to_core)

    def relay_diag(c, t):
        arrive(c, t, 3, 0)
        send(c, t, 3, 7, 1, 3, to_core)

    def finish(c):
        for t in order:
            for o in range(4):
                arrive(1 - c, t, o, 1)

    def drain(c):
        @pl.when(j < last)
        def _():
            for copy in own_copies(c, True):
                copy.wait_send()

        @pl.when(j > 0)
        def _():
            for copy in own_copies(c, False):
                copy.wait_send()

        def sent(t, slot):
            for a, ref in enumerate(piece_from(c, t, 0)):
                remote(ref, ref, wsend.at[t - 1, slot, a], wrecv.at[0, t - 1, 0, a], to_core).wait_send()

        for t in range(1, n_tgt):
            pl.when(((t <= j) & (j < last)) | ((t > j) & (j > 0)))(functools.partial(sent, t, 0))
            for slot in range(1, 8):
                sent(t, slot)

    def by_core(function, *args):
        for c in range(2):
            pl.when(core == c)(functools.partial(function, c, *args))

    feat_own = feat_all.at[pl.ds(pl.multiple_of(j * PAD, PAD), PAD), :]
    feat_sends = [
        remote(feat_own, feat_own, fsend.at[t - 1], frecv.at[t - 1], z_peers[t - 1]) for t in range(1, n_tgt)
    ]
    for copy in feat_sends:
        copy.start()
    by_core(start_z)

    for name in ("to_grid", "ffn", "up", "from_grid_t", "gout", "down", "to_grid_t"):
        staged[name].wait()
    grid_in = mm(to_grid[...], ffn[...]).astype(bf)
    pre = mm(grid_in, up[...])
    value = mm(from_grid_t[...], gout[...]).astype(bf)
    grad_act = mm_nt(value, down[...])
    sig = sigmoid(pre)
    grad_pre = (grad_act * sig * (1.0 + pre * (1.0 - sig))).astype(bf)
    grad_grid = mm_nt(grad_pre, up[...]).astype(bf)
    target = (mm(spread, gout[...]) + mm(to_grid_t[...], grad_grid)).astype(bf)
    targ_all[pl.ds(pl.multiple_of(i * PAD, PAD), PAD), :] = target
    targ_own = targ_all.at[pl.ds(pl.multiple_of(i * PAD, PAD), PAD), :]
    targ_sends = [
        remote(targ_own, targ_own, tsend.at[t - 1], trecv.at[t - 1], plane_peers[t - 1]) for t in range(1, n_src)
    ]
    for copy in targ_sends:
        copy.start()

    by_core(relay_own, order[0])

    for name in ("esrc", "etgt", "eang", "wig"):
        staged[name].wait()
    def iota(shape, axis):
        return lax.broadcasted_iota(jnp.int32, shape, axis)

    eye = (iota((slots, slots), 0) == iota((slots, slots), 1)).astype(bf)
    n_s = n_tgt * PAD
    live = iota((1, slots), 1) < count[...]

    def pick_t(groups, ids):
        index = iota((groups * angles, slots), 0)
        return (index // angles == ids) & (index % angles == eang[...])

    pick_angle_t = (iota((angles, slots), 0) == eang[...]).astype(bf)
    pick_s_t = (pick_t(n_tgt, esrc[...]) & live).astype(bf)
    pick_s = mm_nt(eye, pick_s_t).astype(bf)
    pick_g = mm_nt(eye, pick_t(n_src, etgt[...]).astype(bf)).astype(bf)
    mask_s_t = (iota((n_s, slots), 0) // PAD == esrc[...]) & live
    spread_s_t = (iota((n_s, coef), 0) % PAD == iota((n_s, coef), 1)).astype(bf)
    wig_all = wig[...].reshape(kept * angles, coef)

    for copy in feat_sends:
        copy.wait_recv()
    for n in range(n_tgt):
        table_s[n] = mm(wig_all, feat_all[n * PAD : n * PAD + coef, :]).astype(bf)
    by_core(relay_own, order[1])
    for copy in targ_sends:
        copy.wait_recv()
    for n in range(n_src):
        table_t[n] = mm(wig_all, targ_all[n * PAD : n * PAD + coef, :]).astype(bf)
        if n == n_src // 2:
            by_core(relay, order[0])

    by_core(relay_own, order[2])
    degree_cut = [7, 13, 19, 24, 29]
    for r in range(kept):
        cut = slice(r * angles, (r + 1) * angles)
        row = mm(pick_s, jnp.concatenate([table_s[n, cut, :] for n in range(n_tgt)], axis=0)).astype(bf)
        if r < degree_cut[0]:
            z0[:, r * channels : (r + 1) * channels] = row
        elif r < degree_cut[2]:
            p, at = divmod(r - degree_cut[0], 6)
            z1[p * slots : (p + 1) * slots, at * channels : (at + 1) * channels] = row
        else:
            p, at = divmod(r - degree_cut[2], 5)
            z2[p * slots : (p + 1) * slots, at * channels : (at + 1) * channels] = row
    by_core(relay, order[1])
    by_core(relay_diag, order[0])
    for r in range(kept):
        cut = slice(r * angles, (r + 1) * angles)
        rows = jnp.concatenate([table_t[n, cut, :] for n in range(n_src)], axis=0)
        grad_o[r] = mm(pick_g, rows) * message_scale
    by_core(relay, order[2])
    by_core(relay_diag, order[1])
    for r in range(kept):
        wide = mm_nt(spread_s_t, wig[r]).astype(bf)
        turned = mm(wide, pick_angle_t)
        xs_t[:, r * slots : (r + 1) * slots] = jnp.where(mask_s_t, turned, 0.0).astype(bf)
    by_core(relay_diag, order[2])
    for copy in locals_:
        copy.wait()
    by_core(finish)

    staged["radial"].wait()
    gain = radial[...].astype(f32)
    h0 = mm(z0[...], w0[...])
    for r in range(8):
        hid[r] = h0[:, r * channels : (r + 1) * channels] * gain
    for first, per, zz, ww in ((8, 6, z1, w1), (20, 5, z2, w2)):
        real = mm(zz[...], ww[0])
        imag = mm(zz[...], ww[1])
        plus = real[:slots] - imag[slots:]
        minus = real[slots:] + imag[:slots]
        for r in range(per):
            cut = slice(r * channels, (r + 1) * channels)
            hid[first + r] = plus[:, cut] * gain
            hid[first + per + r] = minus[:, cut] * gain

    sig_gate = sigmoid(hid[7])
    scalar = hid[0]
    sig_scalar = sigmoid(scalar)
    g0[:, :channels] = (grad_o[0] * sig_scalar * (1.0 + scalar * (1.0 - sig_scalar)) * gain).astype(bf)
    gate_gain = sig_gate * gain
    total = jnp.zeros((slots, channels), f32)
    for r in range(1, kept):
        row = grad_o[r]
        total = total + row * hid[r if r < 7 else r + 1]
        value_r = (row * gate_gain).astype(bf)
        if r < 7:
            g0[:, r * channels : (r + 1) * channels] = value_r
        elif r < 19:
            p, at = divmod(r - 7, 6)
            g1[p * slots : (p + 1) * slots, at * channels : (at + 1) * channels] = value_r
        else:
            p, at = divmod(r - 19, 5)
            g2[p * slots : (p + 1) * slots, at * channels : (at + 1) * channels] = value_r
    g0[:, 7 * channels :] = (total * sig_gate * (1.0 - sig_gate) * gain).astype(bf)

    back = mm_nt(g0[...], w0[...]).astype(bf)
    rows = [back[:, r * channels : (r + 1) * channels] for r in range(7)]
    for per, gg, ww in ((6, g1, w1), (5, g2, w2)):
        real = mm_nt(gg[...], ww[0])
        imag = mm_nt(gg[...], ww[1])
        plus = (real[:slots] + imag[slots:]).astype(bf)
        minus = (real[slots:] - imag[:slots]).astype(bf)
        rows += [plus[:, r * channels : (r + 1) * channels] for r in range(per)]
        rows += [minus[:, r * channels : (r + 1) * channels] for r in range(per)]
    part[...] = mm(xs_t[...], jnp.concatenate(rows, axis=0))

    part_sends = [
        remote(
            part.at[pl.ds(pl.multiple_of(((j + t) % n_tgt) * PAD, PAD), PAD), :],
            recv_part.at[t - 1],
            psend.at[t - 1],
            precv.at[t - 1],
            z_peers[t - 1],
        )
        for t in range(1, n_tgt)
    ]
    for copy in part_sends:
        copy.start()
    by_core(drain)
    for copy in feat_sends + targ_sends:
        copy.wait_send()
    summed = part[pl.ds(pl.multiple_of(j * PAD, PAD), PAD), :]
    for t, copy in enumerate(part_sends):
        copy.wait_recv()
        summed = summed + recv_part[t]
    mine = targ_all[pl.ds(pl.multiple_of(i * PAD, PAD), PAD), :].astype(f32)
    out[...] = (mine + summed)[:coef].astype(bf)
    for copy in part_sends:
        copy.wait_send()


def fused_on_device(
    feat_in,
    ffn_in,
    grad_out,
    ffn_up,
    ffn_down,
    so2_zero,
    so2_one,
    so2_two,
    wigner,
    edge_src,
    edge_tgt,
    edge_angle,
    edge_radial,
    edge_count,
):
    n_src, n_tgt = lax.axis_size("src"), lax.axis_size("tgt")
    _, coef, channels = feat_in.shape
    kept = wigner.shape[1]
    slots = edge_src.shape[2]
    to_grid, from_grid = sphere_tables(LMAX, GRID_SIDE)
    more = -to_grid.shape[0] % 16
    to_grid = jnp.pad(to_grid, ((0, more), (0, 0)))
    from_grid_t = jnp.pad(from_grid.T, ((0, more), (0, 0)))
    to_grid_t = jnp.pad(to_grid.T, ((0, PAD - coef), (0, 0)))
    bf, f32 = jnp.bfloat16, jnp.float32
    k0, k1, k2 = so2_zero.shape[0] * n_tgt, so2_one.shape[1] * n_tgt, so2_two.shape[1] * n_tgt
    vmem = pl.BlockSpec(memory_space=pltpu.VMEM)
    hbm = pl.BlockSpec(memory_space=pltpu.HBM)
    dma = pltpu.SemaphoreType.DMA
    first = [
        to_grid,
        from_grid_t,
        to_grid_t,
        feat_in.reshape(coef, channels),
        ffn_in.reshape(coef, channels),
        grad_out.reshape(coef, channels),
        ffn_up,
        ffn_down,
    ]
    second = [
        wigner.transpose(1, 0, 2),
        edge_src.reshape(1, slots),
        edge_tgt.reshape(1, slots),
        edge_angle.reshape(1, slots),
        edge_radial.reshape(slots, channels),
    ]
    result = pl.pallas_call(
        functools.partial(fused_kernel, n_src, n_tgt),
        out_shape=jax.ShapeDtypeStruct((coef, channels), bf),
        in_specs=[hbm] * 16 + [vmem],
        out_specs=vmem,
        scratch_shapes=[pltpu.VMEM(x.shape, x.dtype) for x in first + second]
        + [
            dma((len(first + second),)),
            pltpu.VMEM((k0, so2_zero.shape[1]), bf),
            pltpu.VMEM((2, k1, so2_one.shape[2]), bf),
            pltpu.VMEM((2, k2, so2_two.shape[2]), bf),
            pltpu.VMEM((n_tgt * PAD, channels), bf),
            pltpu.VMEM((n_src * PAD, channels), bf),
            pltpu.VMEM((n_tgt * PAD, channels), f32),
            pltpu.VMEM((n_tgt - 1, PAD, channels), f32),
            pltpu.VMEM((n_tgt, kept * wigner.shape[0], channels), bf),
            pltpu.VMEM((n_src, kept * wigner.shape[0], channels), bf),
            pltpu.VMEM((n_tgt * PAD, kept * slots), bf),
            pltpu.VMEM((slots, k0), bf),
            pltpu.VMEM((2 * slots, k1), bf),
            pltpu.VMEM((2 * slots, k2), bf),
            pltpu.VMEM((kept, slots, channels), f32),
            pltpu.VMEM((kept + 1, slots, channels), f32),
            pltpu.VMEM((slots, so2_zero.shape[1]), bf),
            pltpu.VMEM((2 * slots, k1), bf),
            pltpu.VMEM((2 * slots, k2), bf),
            dma((2, 2)),
            dma((n_tgt - 1, 8, 2)),
            dma((2, n_tgt - 1, 4, 2)),
            dma((3,)),
            dma((n_tgt - 1,)),
            dma((n_tgt - 1,)),
            dma((n_src - 1,)),
            dma((n_src - 1,)),
            dma((n_tgt - 1,)),
            dma((n_tgt - 1,)),
        ],
        compiler_params=pltpu.CompilerParams(
            collective_id=0, has_side_effects=True, vmem_limit_bytes=48 * 1024 * 1024
        ),
    )(
        *first,
        so2_zero,
        so2_one,
        so2_two,
        *second,
        edge_count,
    )
    return result.reshape(feat_in.shape)


def choose(*args):
    if plan_fits(lax.axis_size("src"), lax.axis_size("tgt"), *args[5:8]):
        return fused_on_device(*args)
    return on_device(*args)


def solution(mesh):
    placed = (
        P(("src", "tgt"), None, None),
        P(("src", "tgt"), None, None),
        P(("src", "tgt"), None, None),
        P(),
        P(),
        P("tgt", None),
        P(None, "tgt", None),
        P(None, "tgt", None),
        P(),
        P("src", "tgt", None),
        P("src", "tgt", None),
        P("src", "tgt", None),
        P("src", "tgt", None, None),
        P("src", "tgt"),
    )
    return jax.shard_map(
        choose,
        mesh=mesh,
        in_specs=placed,
        out_specs=P(("src", "tgt"), None, None),
        check_vma=False,
    )
```

```python
import functools
import math

import jax
import jax.numpy as jnp
import numpy as np
from jax import lax
from jax.experimental import pallas as pl
from jax.experimental.pallas import tpu as pltpu
from jax.sharding import PartitionSpec as P

LMAX = 6
GRID_SIDE = 14


message_scale = 0.125


def sphere_tables(degree_max, grid_side):
    polar_angle = (np.arange(grid_side) + 0.5) * np.pi / grid_side
    azimuth = np.arange(grid_side) * 2.0 * np.pi / grid_side
    cosine = np.cos(polar_angle)
    sine_theta = np.sin(polar_angle)
    coef_count = (degree_max + 1) * (degree_max + 1)
    harmonics = np.zeros((grid_side, grid_side, coef_count))
    for order_m in range(degree_max + 1):
        diagonal = np.ones(grid_side)
        for factor in range(1, order_m + 1):
            diagonal = diagonal * (2 * factor - 1) * sine_theta
        legendre = {order_m: diagonal}
        if order_m + 1 <= degree_max:
            legendre[order_m + 1] = cosine * (2 * order_m + 1) * diagonal
        for degree in range(order_m + 2, degree_max + 1):
            legendre[degree] = (
                (2 * degree - 1) * cosine * legendre[degree - 1]
                - (degree + order_m - 1) * legendre[degree - 2]
            ) / (degree - order_m)
        for degree in range(order_m, degree_max + 1):
            scaling = math.sqrt(
                (2 * degree + 1)
                / (4.0 * math.pi)
                * math.factorial(degree - order_m)
                / math.factorial(degree + order_m)
            )
            if order_m > 0:
                scaling = scaling * math.sqrt(2.0)
            polar_part = scaling * legendre[degree]
            centre = degree * degree + degree
            harmonics[:, :, centre + order_m] = (
                polar_part[:, None] * np.cos(order_m * azimuth)[None, :]
            )
            if order_m > 0:
                harmonics[:, :, centre - order_m] = (
                    polar_part[:, None] * np.sin(order_m * azimuth)[None, :]
                )
    to_grid = harmonics.reshape(grid_side * grid_side, coef_count)
    quadrature = np.repeat(sine_theta * (np.pi / grid_side) * (2.0 * np.pi / grid_side), grid_side)
    from_grid = (to_grid * quadrature[:, None]).T
    return (
        jnp.asarray(to_grid, jnp.float32).astype(jnp.bfloat16),
        jnp.asarray(from_grid, jnp.float32).astype(jnp.bfloat16),
    )


def matmul_plain(left, right):
    return jnp.dot(left, right, preferred_element_type=jnp.float32)


def matmul_flip(left, right):
    return lax.dot_general(
        left, right, (((1,), (1,)), ((), ())), preferred_element_type=jnp.float32
    )


def ffn_backward(ffn_rows, grad_rows, ffn_up, ffn_down, to_grid, from_grid):
    atom_count, coef_count, channels = ffn_rows.shape
    grid_feat = jnp.einsum(
        "pk,akc->apc", to_grid, ffn_rows, preferred_element_type=jnp.float32
    ).astype(jnp.bfloat16)
    grid_points = grid_feat.shape[1]
    pre_act = matmul_plain(grid_feat.reshape(atom_count * grid_points, channels), ffn_up)
    grad_value = jnp.einsum(
        "kp,akc->apc", from_grid, grad_rows, preferred_element_type=jnp.float32
    ).astype(jnp.bfloat16)
    grad_act = matmul_flip(grad_value.reshape(atom_count * grid_points, channels), ffn_down)
    sigmoid_pre = jax.nn.sigmoid(pre_act)
    grad_pre = (grad_act * sigmoid_pre * (1.0 + pre_act * (1.0 - sigmoid_pre))).astype(jnp.bfloat16)
    grad_grid = matmul_flip(grad_pre, ffn_up).astype(jnp.bfloat16)
    ffn_term = jnp.einsum(
        "pk,apc->akc",
        to_grid,
        grad_grid.reshape(atom_count, grid_points, channels),
        preferred_element_type=jnp.float32,
    )
    return (grad_rows.astype(jnp.float32) + ffn_term).astype(jnp.bfloat16)


def so2_higher(rotated, w_one, w_two, degree_max, channels):
    cut_a = (degree_max + 1) * channels
    cut_b = cut_a + degree_max * channels
    cut_c = cut_b + degree_max * channels
    cut_d = cut_c + (degree_max - 1) * channels
    one_plus = rotated[:, cut_a:cut_b]
    one_minus = rotated[:, cut_b:cut_c]
    two_plus = rotated[:, cut_c:cut_d]
    two_minus = rotated[:, cut_d:]
    out_one_plus = matmul_plain(one_plus, w_one[0]) - matmul_plain(one_minus, w_one[1])
    out_one_minus = matmul_plain(one_minus, w_one[0]) + matmul_plain(one_plus, w_one[1])
    out_two_plus = matmul_plain(two_plus, w_two[0]) - matmul_plain(two_minus, w_two[1])
    out_two_minus = matmul_plain(two_minus, w_two[0]) + matmul_plain(two_plus, w_two[1])
    return jnp.concatenate([out_one_plus, out_one_minus, out_two_plus, out_two_minus], axis=1)


def so2_forward(rotated, weights, degree_max, channels):
    w_zero, w_one, w_two = weights
    cut_a = (degree_max + 1) * channels
    out_zero = matmul_plain(rotated[:, :cut_a], w_zero)
    return jnp.concatenate(
        [out_zero, so2_higher(rotated, w_one, w_two, degree_max, channels)], axis=1
    )


def so2_backward(grad_pre, weights, degree_max, channels):
    w_zero, w_one, w_two = weights
    cut_a = (degree_max + 2) * channels
    cut_b = cut_a + degree_max * channels
    cut_c = cut_b + degree_max * channels
    cut_d = cut_c + (degree_max - 1) * channels
    grad_zero = grad_pre[:, :cut_a]
    grad_one_plus = grad_pre[:, cut_a:cut_b]
    grad_one_minus = grad_pre[:, cut_b:cut_c]
    grad_two_plus = grad_pre[:, cut_c:cut_d]
    grad_two_minus = grad_pre[:, cut_d:]
    back_zero = matmul_flip(grad_zero, w_zero)
    back_one_plus = matmul_flip(grad_one_plus, w_one[0]) + matmul_flip(grad_one_minus, w_one[1])
    back_one_minus = matmul_flip(grad_one_minus, w_one[0]) - matmul_flip(grad_one_plus, w_one[1])
    back_two_plus = matmul_flip(grad_two_plus, w_two[0]) + matmul_flip(grad_two_minus, w_two[1])
    back_two_minus = matmul_flip(grad_two_minus, w_two[0]) - matmul_flip(grad_two_plus, w_two[1])
    return jnp.concatenate(
        [back_zero, back_one_plus, back_one_minus, back_two_plus, back_two_minus], axis=1
    )


def gate_backward(hidden, grad_o, degree_max):
    gate_index = degree_max + 1
    scalar_pre = hidden[:, 0]
    gate_pre = hidden[:, gate_index]
    sigmoid_gate = jax.nn.sigmoid(gate_pre)
    sigmoid_scalar = jax.nn.sigmoid(scalar_pre)
    grad_scalar = grad_o[:, 0] * sigmoid_scalar * (1.0 + scalar_pre * (1.0 - sigmoid_scalar))
    gated_rows = jnp.concatenate([hidden[:, 1:gate_index], hidden[:, gate_index + 1 :]], axis=1)
    grad_rows = grad_o[:, 1:]
    grad_gate = jnp.sum(grad_rows * gated_rows, axis=1) * sigmoid_gate * (1.0 - sigmoid_gate)
    grad_gated = grad_rows * sigmoid_gate[:, None, :]
    return jnp.concatenate(
        [
            grad_scalar[:, None],
            grad_gated[:, :degree_max],
            grad_gate[:, None],
            grad_gated[:, degree_max:],
        ],
        axis=1,
    )


def on_device(
    feat_in,
    ffn_in,
    grad_out,
    ffn_up,
    ffn_down,
    so2_zero,
    so2_one,
    so2_two,
    wigner,
    edge_src,
    edge_tgt,
    edge_angle,
    edge_radial,
    edge_count,
):
    atom_count, coef_count, channels = feat_in.shape
    angle_bins, kept_rows = (wigner.shape[0], wigner.shape[1])
    slot_total = edge_src.shape[2]
    block_rows = min(128, slot_total)
    to_grid, from_grid = sphere_tables(LMAX, GRID_SIDE)
    source_all = lax.all_gather(feat_in, "tgt", axis=0, tiled=True)
    source_count = source_all.shape[0]
    source_flat = source_all.reshape(source_count, coef_count * channels)
    forward_weights = (
        lax.all_gather(so2_zero, "tgt", axis=0, tiled=True),
        lax.all_gather(so2_one, "tgt", axis=1, tiled=True),
        lax.all_gather(so2_two, "tgt", axis=1, tiled=True),
    )
    target_grad = ffn_backward(ffn_in, grad_out, ffn_up, ffn_down, to_grid, from_grid)
    target_all = lax.all_gather(target_grad, "src", axis=0, tiled=True)
    target_count = target_all.shape[0]
    target_flat = target_all.reshape(target_count, coef_count * channels)
    wigner_flat = wigner.reshape(angle_bins, kept_rows * coef_count)
    src_slots = edge_src.reshape(slot_total)
    tgt_slots = edge_tgt.reshape(slot_total)
    angle_slots = edge_angle.reshape(slot_total)
    radial_slots = edge_radial.reshape(slot_total, channels)
    live_count = edge_count.reshape(())
    source_labels = jnp.arange(source_count, dtype=jnp.int32)
    target_labels = jnp.arange(target_count, dtype=jnp.int32)
    angle_labels = jnp.arange(angle_bins, dtype=jnp.int32)
    block_count = slot_total // block_rows

    def rotate_block():
        pick_source = (src_slots[:, None] == source_labels[None, :]).astype(jnp.bfloat16)
        source_rows = (
            matmul_plain(pick_source, source_flat)
            .astype(jnp.bfloat16)
            .reshape(block_rows, coef_count, channels)
        )
        pick_angle = (angle_slots[:, None] == angle_labels[None, :]).astype(jnp.bfloat16)
        rotation = (
            matmul_plain(pick_angle, wigner_flat)
            .astype(jnp.bfloat16)
            .reshape(block_rows, kept_rows, coef_count)
        )
        rotated = jnp.einsum(
            "erk,ekc->erc", rotation, source_rows, preferred_element_type=jnp.float32
        ).astype(jnp.bfloat16)
        return (rotated.reshape(block_rows, kept_rows * channels), rotation)

    def forward_step(block_index, buffers):
        first_slot = block_index * block_rows
        rotated, rotation = rotate_block()
        hidden = so2_forward(rotated, forward_weights, LMAX, channels)
        hidden = (
            hidden.reshape(block_rows, kept_rows + 1, channels)
            * radial_slots.astype(jnp.float32)[:, None, :]
        )
        hidden_all = hidden.reshape(block_rows, (kept_rows + 1) * channels)
        return (hidden_all, rotation)

    hidden_all, rotation_all = lax.fori_loop(
        0,
        block_count,
        forward_step,
        (
            jnp.zeros((slot_total, (kept_rows + 1) * channels), jnp.float32),
            jnp.zeros((slot_total, kept_rows, coef_count), jnp.bfloat16),
        ),
    )

    def backward_step(block_index, partial_value):
        first_slot = block_index * block_rows
        radial = radial_slots.astype(jnp.float32)
        pick_target = (tgt_slots[:, None] == target_labels[None, :]).astype(jnp.bfloat16)
        target_rows = (
            matmul_plain(pick_target, target_flat)
            .astype(jnp.bfloat16)
            .reshape(block_rows, coef_count, channels)
        )
        hidden = hidden_all.reshape(block_rows, kept_rows + 1, channels)
        grad_o = (
            jnp.einsum(
                "erk,ekc->erc", rotation_all, target_rows, preferred_element_type=jnp.float32
            )
            * message_scale
        )
        grad_hidden = gate_backward(hidden, grad_o, LMAX)
        grad_pre = (
            (grad_hidden * radial[:, None, :])
            .astype(jnp.bfloat16)
            .reshape(block_rows, (kept_rows + 1) * channels)
        )
        grad_rot = (
            so2_backward(grad_pre, forward_weights, LMAX, channels)
            .astype(jnp.bfloat16)
            .reshape(block_rows, kept_rows, channels)
        )
        grad_edge = jnp.einsum(
            "erk,erc->ekc", rotation_all, grad_rot, preferred_element_type=jnp.float32
        ).astype(jnp.bfloat16)
        live_slot = first_slot + jnp.arange(block_rows, dtype=jnp.int32) < live_count
        pick_back = ((src_slots[:, None] == source_labels[None, :]) & live_slot[:, None]).astype(
            jnp.bfloat16
        )
        return partial_value + lax.dot_general(
            pick_back,
            grad_edge.reshape(block_rows, coef_count * channels),
            (((0,), (0,)), ((), ())),
            preferred_element_type=jnp.float32,
        )

    partial_value = lax.fori_loop(
        0, block_count, backward_step, jnp.zeros((source_count, coef_count * channels), jnp.float32)
    )
    summed = lax.psum_scatter(
        partial_value.reshape(source_count, coef_count, channels),
        "tgt",
        scatter_dimension=0,
        tiled=True,
    )
    return (target_grad.astype(jnp.float32) + summed).astype(jnp.bfloat16)


MESH = pl.DeviceIdType.MESH
PAD = 64


def plan_fits(n_src, n_tgt, so2_zero, so2_one, so2_two):
    return (
        n_src == 2**3
        and n_tgt == 2**2
        and so2_zero.shape[0] % 16 == 0
        and so2_zero.shape[1] % 512 == 0
        and so2_one.shape[1] % 32 == 0
        and so2_two.shape[1] % 32 == 0
    )


def mm(left, right):
    return jnp.dot(left, right, preferred_element_type=jnp.float32)


def mm_nt(left, right):
    return lax.dot_general(left, right, (((1,), (1,)), ((), ())), preferred_element_type=jnp.float32)


def sigmoid(value):
    return 1.0 / (1.0 + jnp.exp(-value))


def fused_kernel(
    n_src,
    n_tgt,
    to_grid_in,
    from_grid_t_in,
    to_grid_t_in,
    feat_in,
    ffn_in,
    gout_in,
    up_in,
    down_in,
    w0_in,
    w1_in,
    w2_in,
    wig_in,
    esrc_in,
    etgt_in,
    eang_in,
    radial_in,
    count,
    out,
    to_grid,
    from_grid_t,
    to_grid_t,
    feat,
    ffn,
    gout,
    up,
    down,
    wig,
    esrc,
    etgt,
    eang,
    radial,
    in_sem,
    w0,
    w1,
    w2,
    feat_all,
    targ_all,
    part,
    recv_part,
    table_s,
    table_t,
    xs_t,
    z0,
    z1,
    z2,
    grad_o,
    hid,
    g0,
    g1,
    g2,
    osend,
    wsend,
    wrecv,
    local_sem,
    fsend,
    frecv,
    tsend,
    trecv,
    psend,
    precv,
):
    i = lax.axis_index("src")
    j = lax.axis_index("tgt")
    y, x, core = i // 4, (i // 2) % 2, i % 2
    bf, f32 = jnp.bfloat16, jnp.float32
    coef, channels = feat.shape
    slots = radial.shape[0]
    angles = wig.shape[1]
    kept = wig.shape[0]
    rows0, rows1, rows2 = w0_in.shape[0], w1_in.shape[1], w2_in.shape[1]
    cols0 = w0_in.shape[1] // 4

    def chip_index(yy, xx, cc):
        return yy * 4 + xx * 2 + cc

    to_x = (chip_index(y, 1 - x, core), j)
    to_y = (chip_index(1 - y, x, core), j)
    to_core = (chip_index(y, x, 1 - core), j)
    z_peers = [(i, (j + t) % n_tgt) for t in range(1, n_tgt)]
    plane_peers = [((i + t) % n_src, j) for t in range(1, n_src)]

    staged = {}
    for at, (name, source, target) in enumerate((
        ("feat", feat_in, feat),
        ("ffn", ffn_in, ffn),
        ("gout", gout_in, gout),
        ("to_grid", to_grid_in, to_grid),
        ("from_grid_t", from_grid_t_in, from_grid_t),
        ("up", up_in, up),
        ("down", down_in, down),
        ("to_grid_t", to_grid_t_in, to_grid_t),
        ("esrc", esrc_in, esrc),
        ("etgt", etgt_in, etgt),
        ("eang", eang_in, eang),
        ("wig", wig_in, wig),
        ("radial", radial_in, radial),
    )):
        staged[name] = pltpu.make_async_copy(source, target, in_sem.at[at])
        staged[name].start()

    barrier = pltpu.get_barrier_semaphore()
    for peer in z_peers + plane_peers:
        pl.semaphore_signal(barrier, inc=1, device_id=peer, device_id_type=MESH)

    locals_ = [
        pltpu.make_async_copy(w0_in, w0.at[pl.ds(pl.multiple_of(j * rows0, 16), rows0), :], local_sem.at[0]),
        pltpu.make_async_copy(w1_in, w1.at[:, pl.ds(pl.multiple_of(j * rows1, 16), rows1), :], local_sem.at[1]),
        pltpu.make_async_copy(w2_in, w2.at[:, pl.ds(pl.multiple_of(j * rows2, 16), rows2), :], local_sem.at[2]),
    ]
    for copy in locals_:
        copy.start()

    spread = (
        lax.broadcasted_iota(jnp.int32, (PAD, coef), 0) == lax.broadcasted_iota(jnp.int32, (PAD, coef), 1)
    ).astype(bf)
    staged["feat"].wait()
    feat_all[pl.ds(pl.multiple_of(j * PAD, PAD), PAD), :] = mm(spread, feat[...]).astype(bf)

    pl.semaphore_wait(barrier, len(z_peers) + len(plane_peers))

    def remote(source, target, send, recv, peer):
        return pltpu.make_async_remote_copy(
            src_ref=source, dst_ref=target, send_sem=send, recv_sem=recv, device_id=peer, device_id_type=MESH
        )

    def piece(c, shard, yy, xx):
        if c == 0:
            half = rows1 // 2
            return [w1.at[yy, pl.ds(pl.multiple_of(shard * rows1 + xx * half, 16), half), :]]
        half = rows2 // 2
        return [
            w0.at[
                pl.ds(pl.multiple_of(shard * rows0, 16), rows0),
                pl.ds(pl.multiple_of((yy * 2 + xx) * cols0, 128), cols0),
            ],
            w2.at[yy, pl.ds(pl.multiple_of(shard * rows2 + xx * half, 16), half), :],
        ]

    def own_piece(c):
        if c == 0:
            half = rows1 // 2
            return [w1_in.at[y, pl.ds(pl.multiple_of(x * half, 16), half), :]]
        half = rows2 // 2
        return [
            w0_in.at[:, pl.ds(pl.multiple_of((y * 2 + x) * cols0, 128), cols0)],
            w2_in.at[y, pl.ds(pl.multiple_of(x * half, 16), half), :],
        ]

    def origin(o):
        return (1 - y if o >= 2 else y, 1 - x if o % 2 else x)

    def piece_from(c, t, o):
        yy, xx = origin(o)
        return piece(c, (j + n_tgt - t) % n_tgt, yy, xx)

    last = n_tgt - 1
    lowest, highest = (last - j) // last, j // last
    t_first = 1 + 2 * lowest
    t_third = 2 - lowest + highest
    order = [t_first, 6 - t_first - t_third, t_third]
    above, below = (i, (j + 1) % n_tgt), (i, (j + n_tgt - 1) % n_tgt)

    def own_copies(c, up_way):
        t, peer = (1, above) if up_way else (last, below)
        return [
            remote(source, target, osend.at[int(up_way), a], wrecv.at[0, t - 1, 0, a], peer)
            for a, (source, target) in enumerate(zip(own_piece(c), piece(c, j, y, x)))
        ]

    def start_z(c):
        @pl.when(j < last)
        def _():
            for copy in own_copies(c, True):
                copy.start()

        @pl.when(j > 0)
        def _():
            for copy in own_copies(c, False):
                copy.start()

    def send(c, t, o, slot, kind, to_o, peer):
        for a, ref in enumerate(piece_from(c, t, o)):
            remote(ref, ref, wsend.at[t - 1, slot, a], wrecv.at[kind, t - 1, to_o, a], peer).start()

    def onward(c, t, to_t, peer):
        for a, ref in enumerate(piece_from(c, t, 0)):
            remote(ref, ref, wsend.at[t - 1, 0, a], wrecv.at[0, to_t - 1, 0, a], peer).start()

    def arrive(c, t, o, kind):
        for a, ref in enumerate(piece_from(c, t, o)):
            remote(ref, ref, wsend.at[t - 1, 0, a], wrecv.at[kind, t - 1, o, a], to_core).wait_recv()

    def relay_own(c, t):
        arrive(c, t, 0, 0)

        @pl.when((t <= j) & (j < last))
        def _():
            onward(c, t, t + 1, above)

        @pl.when((t > j) & (j > 0))
        def _():
            onward(c, t, t - 1, below)

        send(c, t, 0, 1, 0, 1, to_x)
        send(c, t, 0, 2, 0, 2, to_y)
        send(c, t, 0, 4, 1, 0, to_core)

    def relay(c, t):
        arrive(c, t, 1, 0)
        if c == 0:
            send(c, t, 1, 3, 0, 3, to_y)
        send(c, t, 1, 5, 1, 1, to_core)
        arrive(c, t, 2, 0)
        if c == 1:
            send(c, t, 2, 3, 0, 3, to_x)
        send(c, t, 2, 6, 1, 2, to_core)

    def relay_diag(c, t):
        arrive(c, t, 3, 0)
        send(c, t, 3, 7, 1, 3, to_core)

    def finish(c):
        for t in order:
            for o in range(4):
                arrive(1 - c, t, o, 1)

    def drain(c):
        @pl.when(j < last)
        def _():
            for copy in own_copies(c, True):
                copy.wait_send()

        @pl.when(j > 0)
        def _():
            for copy in own_copies(c, False):
                copy.wait_send()

        def sent(t, slot):
            for a, ref in enumerate(piece_from(c, t, 0)):
                remote(ref, ref, wsend.at[t - 1, slot, a], wrecv.at[0, t - 1, 0, a], to_core).wait_send()

        for t in range(1, n_tgt):
            pl.when(((t <= j) & (j < last)) | ((t > j) & (j > 0)))(functools.partial(sent, t, 0))
            for slot in range(1, 8):
                sent(t, slot)

    def by_core(function, *args):
        for c in range(2):
            pl.when(core == c)(functools.partial(function, c, *args))

    feat_own = feat_all.at[pl.ds(pl.multiple_of(j * PAD, PAD), PAD), :]
    feat_sends = [
        remote(feat_own, feat_own, fsend.at[t - 1], frecv.at[t - 1], z_peers[t - 1]) for t in range(1, n_tgt)
    ]
    for copy in feat_sends:
        copy.start()
    by_core(start_z)

    for name in ("to_grid", "ffn", "up", "from_grid_t", "gout", "down", "to_grid_t"):
        staged[name].wait()
    grid_in = mm(to_grid[...], ffn[...]).astype(bf)
    pre = mm(grid_in, up[...])
    value = mm(from_grid_t[...], gout[...]).astype(bf)
    grad_act = mm_nt(value, down[...])
    sig = sigmoid(pre)
    grad_pre = (grad_act * sig * (1.0 + pre * (1.0 - sig))).astype(bf)
    grad_grid = mm_nt(grad_pre, up[...]).astype(bf)
    target = (mm(spread, gout[...]) + mm(to_grid_t[...], grad_grid)).astype(bf)
    targ_all[pl.ds(pl.multiple_of(i * PAD, PAD), PAD), :] = target
    targ_own = targ_all.at[pl.ds(pl.multiple_of(i * PAD, PAD), PAD), :]
    targ_sends = [
        remote(targ_own, targ_own, tsend.at[t - 1], trecv.at[t - 1], plane_peers[t - 1]) for t in range(1, n_src)
    ]
    for copy in targ_sends:
        copy.start()

    by_core(relay_own, order[0])

    for name in ("esrc", "etgt", "eang", "wig"):
        staged[name].wait()
    def iota(shape, axis):
        return lax.broadcasted_iota(jnp.int32, shape, axis)

    eye = (iota((slots, slots), 0) == iota((slots, slots), 1)).astype(bf)
    n_s = n_tgt * PAD
    live = iota((1, slots), 1) < count[...]

    def pick_t(groups, ids):
        index = iota((groups * angles, slots), 0)
        return (index // angles == ids) & (index % angles == eang[...])

    pick_angle_t = (iota((angles, slots), 0) == eang[...]).astype(bf)
    pick_s_t = (pick_t(n_tgt, esrc[...]) & live).astype(bf)
    pick_s = mm_nt(eye, pick_s_t).astype(bf)
    pick_g = mm_nt(eye, pick_t(n_src, etgt[...]).astype(bf)).astype(bf)
    mask_s_t = (iota((n_s, slots), 0) // PAD == esrc[...]) & live
    spread_s_t = (iota((n_s, coef), 0) % PAD == iota((n_s, coef), 1)).astype(bf)
    wig_all = wig[...].reshape(kept * angles, coef)

    for copy in feat_sends:
        copy.wait_recv()
    for n in range(n_tgt):
        table_s[n] = mm(wig_all, feat_all[n * PAD : n * PAD + coef, :]).astype(bf)
    by_core(relay_own, order[1])
    for copy in targ_sends:
        copy.wait_recv()
    for n in range(n_src):
        table_t[n] = mm(wig_all, targ_all[n * PAD : n * PAD + coef, :]).astype(bf)
        if n == n_src // 2:
            by_core(relay, order[0])

    by_core(relay_own, order[2])
    degree_cut = [7, 13, 19, 24, 29]
    for r in range(kept):
        cut = slice(r * angles, (r + 1) * angles)
        row = mm(pick_s, jnp.concatenate([table_s[n, cut, :] for n in range(n_tgt)], axis=0)).astype(bf)
        if r < degree_cut[0]:
            z0[:, r * channels : (r + 1) * channels] = row
        elif r < degree_cut[2]:
            p, at = divmod(r - degree_cut[0], 6)
            z1[p * slots : (p + 1) * slots, at * channels : (at + 1) * channels] = row
        else:
            p, at = divmod(r - degree_cut[2], 5)
            z2[p * slots : (p + 1) * slots, at * channels : (at + 1) * channels] = row
    by_core(relay, order[1])
    by_core(relay_diag, order[0])
    for r in range(kept):
        cut = slice(r * angles, (r + 1) * angles)
        rows = jnp.concatenate([table_t[n, cut, :] for n in range(n_src)], axis=0)
        grad_o[r] = mm(pick_g, rows) * message_scale
    by_core(relay, order[2])
    by_core(relay_diag, order[1])
    for r in range(kept):
        wide = mm_nt(spread_s_t, wig[r]).astype(bf)
        turned = mm(wide, pick_angle_t)
        xs_t[:, r * slots : (r + 1) * slots] = jnp.where(mask_s_t, turned, 0.0).astype(bf)
    by_core(relay_diag, order[2])
    for copy in locals_:
        copy.wait()
    by_core(finish)

    staged["radial"].wait()
    gain = radial[...].astype(f32)
    h0 = mm(z0[...], w0[...])
    for r in range(8):
        hid[r] = h0[:, r * channels : (r + 1) * channels] * gain
    for first, per, zz, ww in ((8, 6, z1, w1), (20, 5, z2, w2)):
        real = mm(zz[...], ww[0])
        imag = mm(zz[...], ww[1])
        plus = real[:slots] - imag[slots:]
        minus = real[slots:] + imag[:slots]
        for r in range(per):
            cut = slice(r * channels, (r + 1) * channels)
            hid[first + r] = plus[:, cut] * gain
            hid[first + per + r] = minus[:, cut] * gain

    sig_gate = sigmoid(hid[7])
    scalar = hid[0]
    sig_scalar = sigmoid(scalar)
    g0[:, :channels] = (grad_o[0] * sig_scalar * (1.0 + scalar * (1.0 - sig_scalar)) * gain).astype(bf)
    gate_gain = sig_gate * gain
    total = jnp.zeros((slots, channels), f32)
    for r in range(1, kept):
        row = grad_o[r]
        total = total + row * hid[r if r < 7 else r + 1]
        value_r = (row * gate_gain).astype(bf)
        if r < 7:
            g0[:, r * channels : (r + 1) * channels] = value_r
        elif r < 19:
            p, at = divmod(r - 7, 6)
            g1[p * slots : (p + 1) * slots, at * channels : (at + 1) * channels] = value_r
        else:
            p, at = divmod(r - 19, 5)
            g2[p * slots : (p + 1) * slots, at * channels : (at + 1) * channels] = value_r
    g0[:, 7 * channels :] = (total * sig_gate * (1.0 - sig_gate) * gain).astype(bf)

    back = mm_nt(g0[...], w0[...]).astype(bf)
    rows = [back[:, r * channels : (r + 1) * channels] for r in range(7)]
    for per, gg, ww in ((6, g1, w1), (5, g2, w2)):
        real = mm_nt(gg[...], ww[0])
        imag = mm_nt(gg[...], ww[1])
        plus = (real[:slots] + imag[slots:]).astype(bf)
        minus = (real[slots:] - imag[:slots]).astype(bf)
        rows += [plus[:, r * channels : (r + 1) * channels] for r in range(per)]
        rows += [minus[:, r * channels : (r + 1) * channels] for r in range(per)]
    part[...] = mm(xs_t[...], jnp.concatenate(rows, axis=0))

    part_sends = [
        remote(
            part.at[pl.ds(pl.multiple_of(((j + t) % n_tgt) * PAD, PAD), PAD), :],
            recv_part.at[t - 1],
            psend.at[t - 1],
            precv.at[t - 1],
            z_peers[t - 1],
        )
        for t in range(1, n_tgt)
    ]
    for copy in part_sends:
        copy.start()
    by_core(drain)
    for copy in feat_sends + targ_sends:
        copy.wait_send()
    summed = part[pl.ds(pl.multiple_of(j * PAD, PAD), PAD), :]
    for t, copy in enumerate(part_sends):
        copy.wait_recv()
        summed = summed + recv_part[t]
    mine = targ_all[pl.ds(pl.multiple_of(i * PAD, PAD), PAD), :].astype(f32)
    out[...] = (mine + summed)[:coef].astype(bf)
    for copy in part_sends:
        copy.wait_send()


def fused_on_device(
    feat_in,
    ffn_in,
    grad_out,
    ffn_up,
    ffn_down,
    so2_zero,
    so2_one,
    so2_two,
    wigner,
    edge_src,
    edge_tgt,
    edge_angle,
    edge_radial,
    edge_count,
):
    n_src, n_tgt = lax.axis_size("src"), lax.axis_size("tgt")
    _, coef, channels = feat_in.shape
    kept = wigner.shape[1]
    slots = edge_src.shape[2]
    to_grid, from_grid = sphere_tables(LMAX, GRID_SIDE)
    more = -to_grid.shape[0] % 16
    to_grid = jnp.pad(to_grid, ((0, more), (0, 0)))
    from_grid_t = jnp.pad(from_grid.T, ((0, more), (0, 0)))
    to_grid_t = jnp.pad(to_grid.T, ((0, PAD - coef), (0, 0)))
    bf, f32 = jnp.bfloat16, jnp.float32
    k0, k1, k2 = so2_zero.shape[0] * n_tgt, so2_one.shape[1] * n_tgt, so2_two.shape[1] * n_tgt
    vmem = pl.BlockSpec(memory_space=pltpu.VMEM)
    hbm = pl.BlockSpec(memory_space=pltpu.HBM)
    dma = pltpu.SemaphoreType.DMA
    first = [
        to_grid,
        from_grid_t,
        to_grid_t,
        feat_in.reshape(coef, channels),
        ffn_in.reshape(coef, channels),
        grad_out.reshape(coef, channels),
        ffn_up,
        ffn_down,
    ]
    second = [
        wigner.transpose(1, 0, 2),
        edge_src.reshape(1, slots),
        edge_tgt.reshape(1, slots),
        edge_angle.reshape(1, slots),
        edge_radial.reshape(slots, channels),
    ]
    result = pl.pallas_call(
        functools.partial(fused_kernel, n_src, n_tgt),
        out_shape=jax.ShapeDtypeStruct((coef, channels), bf),
        in_specs=[hbm] * 16 + [vmem],
        out_specs=vmem,
        scratch_shapes=[pltpu.VMEM(x.shape, x.dtype) for x in first + second]
        + [
            dma((len(first + second),)),
            pltpu.VMEM((k0, so2_zero.shape[1]), bf),
            pltpu.VMEM((2, k1, so2_one.shape[2]), bf),
            pltpu.VMEM((2, k2, so2_two.shape[2]), bf),
            pltpu.VMEM((n_tgt * PAD, channels), bf),
            pltpu.VMEM((n_src * PAD, channels), bf),
            pltpu.VMEM((n_tgt * PAD, channels), f32),
            pltpu.VMEM((n_tgt - 1, PAD, channels), f32),
            pltpu.VMEM((n_tgt, kept * wigner.shape[0], channels), bf),
            pltpu.VMEM((n_src, kept * wigner.shape[0], channels), bf),
            pltpu.VMEM((n_tgt * PAD, kept * slots), bf),
            pltpu.VMEM((slots, k0), bf),
            pltpu.VMEM((2 * slots, k1), bf),
            pltpu.VMEM((2 * slots, k2), bf),
            pltpu.VMEM((kept, slots, channels), f32),
            pltpu.VMEM((kept + 1, slots, channels), f32),
            pltpu.VMEM((slots, so2_zero.shape[1]), bf),
            pltpu.VMEM((2 * slots, k1), bf),
            pltpu.VMEM((2 * slots, k2), bf),
            dma((2, 2)),
            dma((n_tgt - 1, 8, 2)),
            dma((2, n_tgt - 1, 4, 2)),
            dma((3,)),
            dma((n_tgt - 1,)),
            dma((n_tgt - 1,)),
            dma((n_src - 1,)),
            dma((n_src - 1,)),
            dma((n_tgt - 1,)),
            dma((n_tgt - 1,)),
        ],
        compiler_params=pltpu.CompilerParams(
            collective_id=0, has_side_effects=True, vmem_limit_bytes=63 * 1024 * 1024
        ),
    )(
        *first,
        so2_zero,
        so2_one,
        so2_two,
        *second,
        edge_count,
    )
    return result.reshape(feat_in.shape)


def choose(*args):
    if plan_fits(lax.axis_size("src"), lax.axis_size("tgt"), *args[5:8]):
        return fused_on_device(*args)
    return on_device(*args)


def solution(mesh):
    placed = (
        P(("src", "tgt"), None, None),
        P(("src", "tgt"), None, None),
        P(("src", "tgt"), None, None),
        P(),
        P(),
        P("tgt", None),
        P(None, "tgt", None),
        P(None, "tgt", None),
        P(),
        P("src", "tgt", None),
        P("src", "tgt", None),
        P("src", "tgt", None),
        P("src", "tgt", None, None),
        P("src", "tgt"),
    )
    return jax.shard_map(
        choose,
        mesh=mesh,
        in_specs=placed,
        out_specs=P(("src", "tgt"), None, None),
        check_vma=False,
    )
```
